512 devices in a mesh: pipe: 16 (over y, x_lo), expert: 16 (over z, core), dp: 2 (over x_hi).
Axes of the slice: x: 4 (x_hi: 2, x_lo: 2; x = x_hi * 2 + x_lo), y: 8, z: 8, core: 2. Of those that a mesh axis runs over, the one named last changes fastest.
Arguments:
- forward_input: bfloat16 [16, 2048, 3584], P('pipe', 'expert', 'dp'), may hold values from -6 to 6
- saved_input: bfloat16 [16, 2048, 3584], P('pipe', 'expert', 'dp'), may hold values from -6 to 6
- output_grad: bfloat16 [16, 2048, 3584], P('pipe', 'expert', 'dp'), may hold values from -6 to 6
- gate_proj: bfloat16 [16, 3584, 4096], P('pipe', 'dp', 'expert'), may hold values from -0.09375 to 0.09375
- up_proj: bfloat16 [16, 3584, 4096], P('pipe', 'dp', 'expert'), may hold values from -0.09375 to 0.09375
- down_proj: bfloat16 [16, 4096, 3584], P('pipe', 'expert', 'dp'), may hold values from -0.125 to 0.125
- affinity: float32 [2, 16, 2048, 8], P(None, 'pipe', 'expert'), may hold values from 0.05 to 1
- token_lists: int32 [2, 16, 16, 2, 16], P(None, 'pipe', 'expert'), may hold values from -1 to 127, as said below
- slot_ids: int32 [2, 16, 16, 2, 16], P(None, 'pipe', 'expert'), may hold values from 0 to 7, as said below
Outputs:
- next_section_input: bfloat16 [16, 2048, 3584], P('pipe', 'expert', 'dp')
- prev_section_grad: bfloat16 [16, 2048, 3584], P('pipe', 'expert', 'dp')
The draws below stay inside these ranges and needn't reach their ends.
Inputs may be any that keep to these rules, and one draw needn't show every extreme that they name: `token_lists`: an entry is an index into the 128 tokens of source index j, or -1. The live entries of one list are distinct and come first, then -1 to the end. In every block and section one expert's lists are full from every source; the others hold 1 to 16 tokens. `slot_ids`: where a token stands in the lists of several experts of one block and section, their slots differ. The entry is 0 where the list entry is -1.
All inputs are finite; a program needn't handle non-finite values.
Results may differ from the reference program's by a relative error of at most 0.0064.
Values may be sent and summed in bfloat16 or wider, within the bound.
A program may use at most 64 MiB of HBM per device.

```python
import math
import jax
import jax.numpy as jnp
from jax import lax

D = 3584
FF = 2048
TOPK = 8
EXPERTS = 2
TOK_DEV = 128
CAP = 16
SECTIONS = 16
SOURCES = 16
GROUPS = 8
TOKENS = 2048


def routing_tables(base_key):
    draw_shape = (2, SECTIONS, SOURCES, EXPERTS)
    count_key, hot_key, score_key, slot_key = jax.random.split(base_key, 4)
    counts = jax.random.randint(count_key, draw_shape, 1, CAP + 1)
    hot_expert = jax.random.randint(hot_key, (2, SECTIONS, 1, 1), 0, EXPERTS)
    expert_ids = jnp.arange(EXPERTS, dtype=jnp.int32)
    counts = jnp.where(expert_ids == hot_expert, CAP, counts)
    scores = jax.random.randint(score_key, draw_shape + (TOK_DEV,), 0, 1 << 20) * TOK_DEV + jnp.arange(TOK_DEV, dtype=jnp.int32)
    chosen = lax.top_k(scores, CAP)[1].astype(jnp.int32)
    positions = jnp.arange(CAP, dtype=jnp.int32)
    live_mask = positions < counts[..., None]
    list_table = jnp.where(live_mask, chosen, -1).astype(jnp.int32)
    slot_base = jax.random.randint(slot_key, (2, SECTIONS, SOURCES, 1, TOK_DEV), 0, TOPK)
    token_base = jnp.take_along_axis(jnp.broadcast_to(slot_base, draw_shape + (TOK_DEV,)), chosen, axis=-1)
    slot_table = jnp.where(live_mask, (token_base + expert_ids[:, None]) % TOPK, 0).astype(jnp.int32)
    return (list_table, slot_table)


def draw_token_lists(key, part):
    return routing_tables(key)[0]


def draw_slot_ids(key, part):
    return routing_tables(key)[1]


def block_scale(stream_key, shape, shards, least, largest):
    level, own = 1.0, jax.random.fold_in(stream_key, 6)
    for dim, blocks in shards:
        draws = jnp.exp(jax.random.uniform(jax.random.fold_in(own, dim), (blocks,), jnp.float32, least / len(shards), largest / len(shards)))
        level = level * jnp.repeat(draws, shape[dim] // blocks).reshape([-1 if axis == dim else 1 for axis in range(len(shape))])
    return level


def bell_draw(rng, extent, spread, bound, cuts=(), held_as=jnp.bfloat16):
    gain = block_scale(rng, extent, cuts, -0.22, 0.18) if cuts else 1.0
    entries = jax.random.normal(rng, extent, jnp.float32) * spread * gain
    return jnp.minimum(jnp.maximum(entries, -bound), bound).astype(held_as)


def setup_inputs(seed: int = 0) -> dict:
    streams_of = jax.random.split(jax.random.key(seed), 10)
    forward_input = bell_draw(streams_of[0], (SECTIONS, TOKENS, D), 1.0, 6.0, ((0, 16), (1, 16), (2, 2)))
    saved_input = bell_draw(streams_of[1], (SECTIONS, TOKENS, D), 1.0, 6.0, ((0, 16), (1, 16), (2, 2)))
    output_grad = bell_draw(streams_of[2], (SECTIONS, TOKENS, D), 1.0, 6.0, ((0, 16), (1, 16), (2, 2)))
    gate_proj = bell_draw(streams_of[3], (SECTIONS, D, EXPERTS * FF), D ** -0.5, 0.09375, ((0, 16), (1, 2), (2, 16)))
    up_proj = bell_draw(streams_of[4], (SECTIONS, D, EXPERTS * FF), D ** -0.5, 0.09375, ((0, 16), (1, 2), (2, 16)))
    down_proj = bell_draw(streams_of[5], (SECTIONS, EXPERTS * FF, D), FF ** -0.5, 0.125, ((0, 16), (1, 16), (2, 2)))
    affinity = jnp.clip(jnp.exp(math.log(1.0) - 2.9957323 * jax.random.uniform(streams_of[6], (2, SECTIONS, TOKENS, TOPK), jnp.float32) ** block_scale(streams_of[6], (2, SECTIONS, TOKENS, TOPK), ((1, 16), (2, 16)), -0.2, 0.2)), 0.05, 1.0)
    token_lists = draw_token_lists(jax.random.fold_in(streams_of[9], 71), 0)
    slot_ids = draw_slot_ids(jax.random.fold_in(streams_of[9], 71), 0)
    return dict(forward_input=forward_input, saved_input=saved_input, output_grad=output_grad, gate_proj=gate_proj, up_proj=up_proj, down_proj=down_proj, affinity=affinity, token_lists=token_lists, slot_ids=slot_ids)


ROUTED_SCALE = 2.5
HIGHEST_PRECISION = lax.Precision.HIGHEST


def entry_index(token_list):
    offsets = (jnp.arange(SOURCES, dtype=jnp.int32) * TOK_DEV)[:, None, None]
    live_mask = token_list >= 0
    take_index = jnp.where(live_mask, token_list + offsets, 0).astype(jnp.int32)
    drop_index = jnp.where(live_mask, token_list + offsets, TOKENS).astype(jnp.int32)
    return live_mask, take_index, drop_index


def route_weights(section_affinity, live_mask, take_index, slot_list):
    normalized = section_affinity / jnp.sum(section_affinity, axis=1, keepdims=True)
    return jnp.where(live_mask, ROUTED_SCALE * normalized[take_index, slot_list], jnp.float32(0.0))


def take_rows(source, live_mask, take_index):
    picked = source[take_index]
    return jnp.where(live_mask[..., None], picked, jnp.zeros_like(picked))


def project_in(picked, w_gate, w_up):
    rows_float = picked.astype(jnp.float32)
    gate_part = jnp.einsum("jekd,edf->jekf", rows_float, w_gate, precision=HIGHEST_PRECISION)
    up_part = jnp.einsum("jekd,edf->jekf", rows_float, w_up, precision=HIGHEST_PRECISION)
    return gate_part, up_part


def split_groups(values):
    return values.reshape(values.shape[0], values.shape[1], values.shape[2], GROUPS, FF // GROUPS)


def round_and_add(group_parts):
    rounded = lax.optimization_barrier(group_parts.astype(jnp.bfloat16))
    return jnp.sum(rounded.astype(jnp.float32), axis=3)


def place_rows(values, drop_index):
    flat_rows = values.reshape(-1, D)
    total = jnp.zeros((TOKENS, D), jnp.float32)
    return total.at[drop_index.reshape(-1)].add(flat_rows, mode="drop")


def section_work(packed):
    section_forward, section_saved, section_grad, gate_flat, up_flat, down_flat, section_affinity, section_lists, section_slots = packed
    live_fwd, take_fwd, drop_fwd = entry_index(section_lists[0])
    live_bwd, take_bwd, drop_bwd = entry_index(section_lists[1])
    weight_fwd = route_weights(section_affinity[0], live_fwd, take_fwd, section_slots[0])
    weight_bwd = route_weights(section_affinity[1], live_bwd, take_bwd, section_slots[1])
    w_gate = jnp.transpose(gate_flat.astype(jnp.float32).reshape(D, EXPERTS, FF), (1, 0, 2))
    w_up = jnp.transpose(up_flat.astype(jnp.float32).reshape(D, EXPERTS, FF), (1, 0, 2))
    w_down = down_flat.astype(jnp.float32).reshape(EXPERTS, FF, D)
    down_groups = w_down.reshape(EXPERTS, GROUPS, FF // GROUPS, D)
    gate_groups = w_gate.reshape(EXPERTS, D, GROUPS, FF // GROUPS)
    up_groups = w_up.reshape(EXPERTS, D, GROUPS, FF // GROUPS)

    rows_fwd = take_rows(section_forward, live_fwd, take_fwd)
    gate_fwd, up_fwd = project_in(rows_fwd, w_gate, w_up)
    hidden_fwd = (jax.nn.silu(gate_fwd) * up_fwd).astype(jnp.bfloat16)
    group_parts = jnp.einsum("jekgf,egfd->jekgd", split_groups(hidden_fwd.astype(jnp.float32)), down_groups, precision=HIGHEST_PRECISION)
    expert_out = round_and_add(group_parts)
    layer_out = place_rows(weight_fwd[..., None] * expert_out, drop_fwd).astype(jnp.bfloat16)

    rows_bwd = take_rows(section_saved, live_bwd, take_bwd)
    grad_rows = (weight_bwd[..., None] * take_rows(section_grad, live_bwd, take_bwd).astype(jnp.float32)).astype(jnp.bfloat16)
    gate_bwd, up_bwd = project_in(rows_bwd, w_gate, w_up)
    grad_hidden = jnp.einsum("jekd,efd->jekf", grad_rows.astype(jnp.float32), w_down, precision=HIGHEST_PRECISION)
    sigma_gate = jax.nn.sigmoid(gate_bwd)
    grad_gate = (grad_hidden * up_bwd * sigma_gate * (1.0 + gate_bwd * (1.0 - sigma_gate))).astype(jnp.bfloat16)
    grad_up = (grad_hidden * gate_bwd * sigma_gate).astype(jnp.bfloat16)
    group_parts = jnp.einsum("jekgf,edgf->jekgd", split_groups(grad_gate.astype(jnp.float32)), gate_groups, precision=HIGHEST_PRECISION)
    group_parts = group_parts + jnp.einsum("jekgf,edgf->jekgd", split_groups(grad_up.astype(jnp.float32)), up_groups, precision=HIGHEST_PRECISION)
    grad_rows_in = round_and_add(group_parts)
    input_grad = place_rows(grad_rows_in, drop_bwd).astype(jnp.bfloat16)
    return layer_out, input_grad


def reference(forward_input, saved_input, output_grad, gate_proj, up_proj, down_proj, affinity, token_lists, slot_ids):
    packed = (forward_input, saved_input, output_grad, gate_proj, up_proj, down_proj,
              jnp.moveaxis(affinity, 1, 0), jnp.moveaxis(token_lists, 1, 0), jnp.moveaxis(slot_ids, 1, 0))
    layer_out, input_grad = lax.map(section_work, packed)
    next_section_input = jnp.roll(layer_out, 1, axis=0)
    prev_section_grad = jnp.roll(input_grad, -1, axis=0)
    return next_section_input, prev_section_grad
```

```python
import functools

import jax
import jax.numpy as jnp
from jax import lax
from jax.experimental import pallas as pl
from jax.experimental.pallas import tpu as pltpu
from jax.sharding import PartitionSpec as P

MESH = pl.DeviceIdType.MESH
F32, BF16, I32 = jnp.float32, jnp.bfloat16, jnp.int32
ROUTED_SCALE = 2.5
EXPERTS = 2
CAP = 16
TOK = 128
CHIPS = 8
HALF = 4
FF = 256
ORDER = (1, 7, 2, 6, 3, 5, 4)


def dot(a, b, dims, precision=None):
    return lax.dot_general(a, b, ((dims[0], dims[1]), ((), ())), precision=precision, preferred_element_type=F32)


def column(row):
    wide = jnp.broadcast_to(row.astype(F32), (CAP, CAP))
    eye = lax.broadcasted_iota(I32, (CAP, CAP), 0) == lax.broadcasted_iota(I32, (CAP, CAP), 1)
    return jnp.sum(jnp.where(eye, wide, 0.0), axis=1, keepdims=True)


def picker(row):
    lanes = lax.broadcasted_iota(I32, (CAP, TOK), 1).astype(F32)
    return jnp.where(lanes == column(row), 1.0, 0.0)


def placer(row):
    tokens = lax.broadcasted_iota(I32, (TOK, CAP), 0)
    return jnp.where(tokens == jnp.broadcast_to(row, (TOK, CAP)), 1.0, 0.0)


def entry_weight(onehot, slot_row, affinity):
    picked = dot(onehot, affinity, ((1,), (1,)), lax.Precision.HIGHEST)
    slots = lax.broadcasted_iota(I32, (CAP, CHIPS), 1).astype(F32)
    chosen = jnp.sum(jnp.where(slots == column(slot_row), picked, 0.0), axis=1, keepdims=True)
    total = jnp.sum(picked, axis=1, keepdims=True)
    live = total > 0.0
    return jnp.where(live, ROUTED_SCALE * (chosen / jnp.where(live, total, 1.0)), 0.0)


def kernel(
    fin, sav, gra, wg_h, wu_h, wd_h, aff, lists, slots,
    out_f, out_b,
    vx, wgu, wd, snd, rcv, lst, nlst,
    part_f, part_b, part_g, xs_gu, xr_gu, xs_g, xr_g,
    hid, sib_s, sib_r, own, com_s, com_r, pip_s, pip_r, placed,
    load_sem, store_sem, dis_s, dis_r, fwd_s, fwd_r, dp_s, dp_r, ss_s, ss_r, co_s, co_r, pi_s, pi_r, li_s, li_r,
):
    p, x, d = lax.axis_index("pipe"), lax.axis_index("expert"), lax.axis_index("dp")
    pipes = lax.axis_size("pipe")
    z, c = lax.div(x, 2), lax.rem(x, 2)
    half = lax.div(z, HALF)
    sibling = (p, z * 2 + 1 - c, d)
    partner = (p, x, 1 - d)
    after = (lax.rem(p + 1, pipes), x, d)
    before = (lax.rem(p + pipes - 1, pipes), x, d)
    ahead = lambda k: lax.rem(z + k, CHIPS)
    behind = lambda k: lax.rem(z + CHIPS - k, CHIPS)
    at_chip = lambda zz: (p, zz * 2 + c, d)
    sent = []

    barrier = pltpu.get_barrier_semaphore()
    for peer in [at_chip(ahead(k)) for k in ORDER] + [sibling, partner, after, before]:
        pl.semaphore_signal(barrier, inc=1, device_id=peer, device_id_type=MESH)

    loads = [
        pltpu.make_async_copy(src, dst, load_sem.at[i])
        for i, (src, dst) in enumerate([
            (fin.at[0], vx.at[0]), (sav.at[0], vx.at[1]), (gra.at[0], vx.at[2]),
            (wg_h.at[0], wgu.at[:, pl.ds(0, FF)]), (wu_h.at[0], wgu.at[:, pl.ds(FF, FF)]), (wd_h.at[0], wd),
        ])
    ]
    for load in loads:
        load.start()

    def remote(src, dst, send_sem, recv_sem, device):
        return pltpu.make_async_remote_copy(
            src_ref=src, dst_ref=dst, send_sem=send_sem, recv_sem=recv_sem, device_id=device, device_id_type=MESH
        )

    def send(*args):
        copy = remote(*args)
        copy.start()
        sent.append(copy)

    rows = [[lists[f, 0, 0, pl.ds(e, 1), :] for e in range(EXPERTS)] for f in range(2)]
    slot_rows = [[slots[f, 0, 0, pl.ds(e, 1), :] for e in range(EXPERTS)] for f in range(2)]
    picks = [[picker(rows[f][e]) for e in range(EXPERTS)] for f in range(2)]
    weights = [[entry_weight(picks[f][e], slot_rows[f][e], aff[f, 0]) for e in range(EXPERTS)] for f in range(2)]
    lst[...] = jnp.zeros_like(lst)
    for f in range(2):
        lst[f, pl.ds(0, EXPERTS), pl.ds(0, CAP)] = lists[f, 0, 0]
    pick = [jnp.concatenate(picks[f], axis=0).astype(BF16) for f in range(2)]

    def gather(a):
        f = 0 if a == 0 else 1
        loads[a].wait()
        got = dot(pick[f], vx[a], ((1,), (0,)))
        for e in range(EXPERTS):
            block = got[e * CAP : (e + 1) * CAP]
            if a == 2:
                block = weights[1][e] * block
            snd[a, e] = block.astype(BF16)
        rcv[a, c * CHIPS + z] = snd[a, half]

    def dispatch(a):
        send(rcv.at[a, c * CHIPS + z], rcv.at[a, c * CHIPS + z], fwd_s.at[a, 0], fwd_r.at[a, 0], sibling)
        for k in ORDER:
            send(
                snd.at[a, lax.div(ahead(k), HALF)], rcv.at[a, c * CHIPS + z],
                dis_s.at[a, k], dis_r.at[a, k], at_chip(ahead(k)),
            )

    def forward(a):
        for k in ORDER:
            slot = c * CHIPS + behind(k)
            remote(snd.at[a, 0], rcv.at[a, slot], dis_s.at[a, k], dis_r.at[a, k], sibling).wait_recv()
            send(rcv.at[a, slot], rcv.at[a, slot], fwd_s.at[a, k], fwd_r.at[a, k], sibling)
        for k in (0,) + ORDER:
            slot = (1 - c) * CHIPS + behind(k)
            remote(snd.at[a, 0], rcv.at[a, slot], fwd_s.at[a, k], fwd_r.at[a, k], sibling).wait_recv()

    def all_rows(a):
        return rcv[a].reshape(2 * CHIPS * CAP, rcv.shape[-1])

    gather(0)
    pl.semaphore_wait(barrier, len(ORDER) + 4)
    dispatch(0)
    gather(1)
    dispatch(1)
    gather(2)
    dispatch(2)
    send(lst.at[0], nlst.at[0], li_s.at[0], li_r.at[0], after)
    send(lst.at[1], nlst.at[1], li_s.at[1], li_r.at[1], before)
    for load in loads[3:]:
        load.wait()

    def exchange_gu(f):
        part = part_f if f == 0 else part_b
        got = dot(all_rows(f), wgu[...], ((1,), (0,)))
        part[...] = got
        xs_gu[f] = got.astype(BF16)
        send(xs_gu.at[f], xr_gu.at[f], dp_s.at[f], dp_r.at[f], partner)

    def joined_gu(f):
        part = part_f if f == 0 else part_b
        remote(xs_gu.at[f], xr_gu.at[f], dp_s.at[f], dp_r.at[f], partner).wait_recv()
        total = part[...] + xr_gu[f].astype(F32)
        return total[:, :FF], total[:, FF:]

    def back(f, hidden):
        hid[f, :, :, pl.ds(0, hidden.shape[-1])] = hidden.reshape(2, CHIPS * CAP, hidden.shape[-1])

    def product(f, core):
        if f == 0:
            return dot(hid[0, core, :, pl.ds(0, FF)], wd[...], ((1,), (0,)))
        return dot(hid[1, core], wgu[...], ((1,), (1,)))

    def to_sibling(f):
        sib_s[f] = product(f, 1 - c).astype(BF16).reshape(CHIPS, CAP, wd.shape[-1])
        send(sib_s.at[f], sib_r.at[f], ss_s.at[f], ss_r.at[f], sibling)
        own[f] = product(f, c).reshape(CHIPS, CAP, wd.shape[-1])

    def combine(f):
        remote(sib_s.at[f], sib_r.at[f], ss_s.at[f], ss_r.at[f], sibling).wait_recv()
        com_s[f] = (own[f] + sib_r[f].astype(F32)).astype(BF16)
        com_r[f, z] = com_s[f, z]
        for k in ORDER:
            send(com_s.at[f, ahead(k)], com_r.at[f, z], co_s.at[f, k], co_r.at[f, k], at_chip(ahead(k)))

    def hand_on(f):
        for k in ORDER:
            remote(com_s.at[f, 0], com_r.at[f, behind(k)], co_s.at[f, k], co_r.at[f, k], sibling).wait_recv()
        for e in range(EXPERTS):
            total = jnp.sum(com_r[f, pl.ds(e * HALF, HALF)].astype(F32), axis=0)
            if f == 0:
                total = weights[0][e] * total
            pip_s[f, e] = total.astype(BF16)
        send(pip_s.at[f], pip_r.at[f], pi_s.at[f], pi_r.at[f], after if f == 0 else before)

    def place(f):
        toward = after if f == 0 else before
        remote(lst.at[f], nlst.at[f], li_s.at[f], li_r.at[f], toward).wait_recv()
        remote(pip_s.at[f], pip_r.at[f], pi_s.at[f], pi_r.at[f], toward).wait_recv()
        total = None
        for e in range(EXPERTS):
            spot = placer(nlst[f, pl.ds(e, 1), pl.ds(0, CAP)]).astype(BF16)
            term = dot(spot, pip_r[f, e], ((1,), (0,)))
            total = term if total is None else total + term
        placed[f] = total.astype(BF16)
        copy = pltpu.make_async_copy(placed.at[f], (out_f if f == 0 else out_b).at[0], store_sem.at[f])
        copy.start()
        return copy

    forward(0)
    exchange_gu(0)
    gate, up = joined_gu(0)
    back(0, (gate * jax.nn.sigmoid(gate) * up).astype(BF16))
    to_sibling(0)
    forward(1)
    combine(0)
    exchange_gu(1)
    forward(2)
    part_g[...] = dot(all_rows(2), wd[...], ((1,), (1,)))
    xs_g[...] = part_g[...].astype(BF16)
    send(xs_g, xr_g, dp_s.at[2], dp_r.at[2], partner)
    gate, up = joined_gu(1)
    sg = jax.nn.sigmoid(gate)
    remote(xs_g, xr_g, dp_s.at[2], dp_r.at[2], partner).wait_recv()
    grad = part_g[...] + xr_g[...].astype(F32)
    grad_gate = (grad * up * sg * (1.0 + gate * (1.0 - sg))).astype(BF16)
    grad_up = (grad * gate * sg).astype(BF16)
    back(1, jnp.concatenate([grad_gate, grad_up], axis=1))
    to_sibling(1)
    hand_on(0)
    combine(1)
    first = place(0)
    hand_on(1)
    second = place(1)
    for copy in sent:
        copy.wait_send()
    first.wait()
    second.wait()


def per_device(forward_input, saved_input, output_grad, gate_proj, up_proj, down_proj, affinity, token_lists, slot_ids):
    width = forward_input.shape[-1]
    whole = pl.BlockSpec(memory_space=pl.ANY)
    small = pl.BlockSpec(memory_space=pltpu.VMEM)
    blocks = 2 * CHIPS
    entries = blocks * CAP
    dma = pltpu.SemaphoreType.DMA
    return pl.pallas_call(
        kernel,
        out_shape=(jax.ShapeDtypeStruct((1, TOK, width), BF16),) * 2,
        in_specs=[whole] * 6 + [small] * 3,
        out_specs=(whole, whole),
        scratch_shapes=[
            pltpu.VMEM((3, TOK, width), BF16),
            pltpu.VMEM((width, 2 * FF), BF16),
            pltpu.VMEM((FF, width), BF16),
            pltpu.VMEM((3, EXPERTS, CAP, width), BF16),
            pltpu.VMEM((3, blocks, CAP, width), BF16),
            pltpu.VMEM((2, 8, 128), I32),
            pltpu.VMEM((2, 8, 128), I32),
            pltpu.VMEM((entries, 2 * FF), F32),
            pltpu.VMEM((entries, 2 * FF), F32),
            pltpu.VMEM((entries, FF), F32),
            pltpu.VMEM((2, entries, 2 * FF), BF16),
            pltpu.VMEM((2, entries, 2 * FF), BF16),
            pltpu.VMEM((entries, FF), BF16),
            pltpu.VMEM((entries, FF), BF16),
            pltpu.VMEM((2, 2, CHIPS * CAP, 2 * FF), BF16),
            pltpu.VMEM((2, CHIPS, CAP, width), BF16),
            pltpu.VMEM((2, CHIPS, CAP, width), BF16),
            pltpu.VMEM((2, CHIPS, CAP, width), F32),
            pltpu.VMEM((2, CHIPS, CAP, width), BF16),
            pltpu.VMEM((2, CHIPS, CAP, width), BF16),
            pltpu.VMEM((2, EXPERTS, CAP, width), BF16),
            pltpu.VMEM((2, EXPERTS, CAP, width), BF16),
            pltpu.VMEM((2, TOK, width), BF16),
            dma((6,)), dma((2,)),
            dma((3, CHIPS)), dma((3, CHIPS)), dma((3, CHIPS)), dma((3, CHIPS)),
            dma((3,)), dma((3,)), dma((2,)), dma((2,)),
            dma((2, CHIPS)), dma((2, CHIPS)), dma((2,)), dma((2,)), dma((2,)), dma((2,)),
        ],
        compiler_params=pltpu.CompilerParams(
            collective_id=0, has_side_effects=True, vmem_limit_bytes=48 * 1024 * 1024
        ),
        cost_estimate=pl.CostEstimate(flops=2_000_000_000, bytes_accessed=6_000_000, transcendentals=262_144),
    )(
        forward_input, saved_input, output_grad, gate_proj, up_proj, down_proj,
        jnp.swapaxes(affinity, 2, 3), token_lists, slot_ids,
    )


def solution(mesh):
    in_specs = (
        P("pipe", "expert", "dp"),
        P("pipe", "expert", "dp"),
        P("pipe", "expert", "dp"),
        P("pipe", "dp", "expert"),
        P("pipe", "dp", "expert"),
        P("pipe", "expert", "dp"),
        P(None, "pipe", "expert", None),
        P(None, "pipe", "expert", None, None),
        P(None, "pipe", "expert", None, None),
    )
    out_specs = (P("pipe", "expert", "dp"), P("pipe", "expert", "dp"))
    return jax.shard_map(
        per_device, mesh=mesh, in_specs=in_specs, out_specs=out_specs, check_vma=False
    )
```

```python
import functools

import jax
import jax.numpy as jnp
from jax import lax
from jax.experimental import pallas as pl
from jax.experimental.pallas import tpu as pltpu
from jax.sharding import PartitionSpec as P

MESH = pl.DeviceIdType.MESH
F32, BF16, I32 = jnp.float32, jnp.bfloat16, jnp.int32
ROUTED_SCALE = 2.5
EXPERTS = 2
CAP = 16
TOK = 128
CHIPS = 8
HALF = 4
FF = 256
VMEM_LIMIT = 62 * 1024 * 1024
STEPS = (3, 2, 1)
PEERS = (1, 2, 3, 4, -1, -2, -3)


def dot(a, b, dims, precision=None):
    return lax.dot_general(a, b, ((dims[0], dims[1]), ((), ())), precision=precision, preferred_element_type=F32)


def column(row):
    wide = jnp.broadcast_to(row.astype(F32), (CAP, CAP))
    eye = lax.broadcasted_iota(I32, (CAP, CAP), 0) == lax.broadcasted_iota(I32, (CAP, CAP), 1)
    return jnp.sum(jnp.where(eye, wide, 0.0), axis=1, keepdims=True)


def picker(row):
    lanes = lax.broadcasted_iota(I32, (CAP, TOK), 1).astype(F32)
    return jnp.where(lanes == column(row), 1.0, 0.0)


def placer(row):
    tokens = lax.broadcasted_iota(I32, (TOK, CAP), 0)
    return jnp.where(tokens == jnp.broadcast_to(row, (TOK, CAP)), 1.0, 0.0)


def entry_weight(onehot, slot_row, affinity):
    picked = dot(onehot, affinity, ((1,), (1,)), lax.Precision.HIGHEST)
    slots = lax.broadcasted_iota(I32, (CAP, CHIPS), 1).astype(F32)
    chosen = jnp.sum(jnp.where(slots == column(slot_row), picked, 0.0), axis=1, keepdims=True)
    total = jnp.sum(picked, axis=1, keepdims=True)
    live = total > 0.0
    return jnp.where(live, ROUTED_SCALE * (chosen / jnp.where(live, total, 1.0)), 0.0)


def kernel(
    fin, sav, gra, wg_h, wu_h, wd_h, aff_h, lists_h, slots_h,
    out_f, out_b,
    aff, lists, slots, vx, wgu, wd, snd, rcv, lst, nlst,
    part_f, part_b, part_g, xs_gu, xr_gu, xs_g, xr_g,
    hid, sib_s, sib_r, own, mate_s, mate_r, com_s, com_r, pip_s, pip_r, placed,
    load_sem, store_sem, dis_s, dis_r, fwd_s, fwd_r, dp_s, dp_r, ss_s, ss_r, ma_s, ma_r, co_s, co_r, pi_s, pi_r, li_s, li_r,
):
    p, x, d = lax.axis_index("pipe"), lax.axis_index("expert"), lax.axis_index("dp")
    pipes = lax.axis_size("pipe")
    z, c = lax.div(x, 2), lax.rem(x, 2)
    half = lax.div(z, HALF)
    sibling = (p, z * 2 + 1 - c, d)
    partner = (p, x, 1 - d)
    after = (lax.rem(p + 1, pipes), x, d)
    before = (lax.rem(p + pipes - 1, pipes), x, d)
    toward = 2 * lax.rem(z, 2) - 1
    chip = lambda k: lax.rem(z + CHIPS + k * toward, CHIPS)
    at_chip = lambda k: (p, chip(k) * 2 + c, d)
    goal = {1: 1, 2: -2, 3: 3}
    sent = []

    barrier = pltpu.get_barrier_semaphore()
    for peer in [at_chip(k) for k in PEERS] + [sibling, partner, after, before]:
        pl.semaphore_signal(barrier, inc=1, device_id=peer, device_id_type=MESH)

    loads = [
        pltpu.make_async_copy(src, dst, load_sem.at[i])
        for i, (src, dst) in enumerate([
            (fin.at[0], vx.at[0]), (sav.at[0], vx.at[1]), (gra.at[0], vx.at[2]),
            (wg_h.at[0], wgu.at[:, pl.ds(0, FF)]), (wu_h.at[0], wgu.at[:, pl.ds(FF, FF)]), (wd_h.at[0], wd),
        ])
    ]
    loads += [
        pltpu.make_async_copy(src, dst, load_sem.at[6 + i])
        for i, (src, dst) in enumerate([(lists_h, lists), (slots_h, slots), (aff_h, aff)])
    ]
    for i in (6, 7, 8, 0, 1, 2, 3, 4, 5):
        loads[i].start()

    def remote(src, dst, send_sem, recv_sem, device):
        return pltpu.make_async_remote_copy(
            src_ref=src, dst_ref=dst, send_sem=send_sem, recv_sem=recv_sem, device_id=device, device_id_type=MESH
        )

    def send(*args):
        copy = remote(*args)
        copy.start()
        sent.append(copy)

    for i in (6, 7, 8):
        loads[i].wait()
    rows = [[lists[f, 0, 0, pl.ds(e, 1), :] for e in range(EXPERTS)] for f in range(2)]
    slot_rows = [[slots[f, 0, 0, pl.ds(e, 1), :] for e in range(EXPERTS)] for f in range(2)]
    picks = [[picker(rows[f][e]) for e in range(EXPERTS)] for f in range(2)]
    weights = [[entry_weight(picks[f][e], slot_rows[f][e], aff[f, 0]) for e in range(EXPERTS)] for f in range(2)]
    lst[...] = jnp.zeros_like(lst)
    for f in range(2):
        lst[f, pl.ds(0, EXPERTS), pl.ds(0, CAP)] = lists[f, 0, 0]
    pick = [jnp.concatenate(picks[f], axis=0).astype(BF16) for f in range(2)]

    def gather(a):
        f = 0 if a == 0 else 1
        loads[a].wait()
        got = dot(pick[f], vx[a], ((1,), (0,)))
        for e in range(EXPERTS):
            block = got[e * CAP : (e + 1) * CAP]
            if a == 2:
                block = weights[1][e] * block
            snd[a, e] = block.astype(BF16)
        rcv[a, c * CHIPS + z] = snd[a, half]

    def slot_of(k, core=None):
        return (c if core is None else core) * CHIPS + chip(k)

    def dispatch(a):
        for k in STEPS:
            send(
                snd.at[a, lax.div(chip(goal[k]), HALF)], rcv.at[a, slot_of(0)],
                dis_s.at[a, k], dis_r.at[a, k], at_chip(goal[k]),
            )
        send(snd.at[a, half], rcv.at[a, slot_of(0)], dis_s.at[a, 0], dis_r.at[a, 0], at_chip(-1))
        share(a, 0, 0)

    def share(a, k, i):
        send(rcv.at[a, slot_of(k)], rcv.at[a, slot_of(k)], fwd_s.at[a, i], fwd_r.at[a, i], sibling)

    def arrived(a, k, i, sems=None, core=None):
        remote(snd.at[a, 0], rcv.at[a, slot_of(k, core)], dis_s.at[a, i], (dis_r if sems is None else sems).at[a, i], sibling).wait_recv()

    def relay(a):
        for k in (1, 2, 3):
            arrived(a, k, k)
            send(rcv.at[a, slot_of(k)], rcv.at[a, slot_of(k)], dis_s.at[a, 4 + k], dis_r.at[a, 4 + k], at_chip(-1))
            share(a, k, k)

    def collect(a):
        arrived(a, -1, 0)
        share(a, -1, 4)
        for k in (1, 2, 3):
            arrived(a, -1 - k, 4 + k)
            share(a, -1 - k, 4 + k)
        for k, i in ((0, 0), (1, 1), (2, 2), (3, 3), (-1, 4), (-2, 5), (-3, 6), (-4, 7)):
            arrived(a, k, i, fwd_r, 1 - c)

    def all_rows(a):
        return rcv[a].reshape(2 * CHIPS * CAP, rcv.shape[-1])

    gather(0)
    gather(1)
    pl.semaphore_wait(barrier, len(PEERS) + 4)
    dispatch(0)
    dispatch(1)
    gather(2)
    dispatch(2)
    send(lst.at[0], nlst.at[0], li_s.at[0], li_r.at[0], after)
    send(lst.at[1], nlst.at[1], li_s.at[1], li_r.at[1], before)
    for load in loads[3:6]:
        load.wait()

    def exchange_gu(f):
        part = part_f if f == 0 else part_b
        got = dot(all_rows(f), wgu[...], ((1,), (0,)))
        part[...] = got
        xs_gu[f] = got.astype(BF16)
        send(xs_gu.at[f], xr_gu.at[f], dp_s.at[f], dp_r.at[f], partner)

    def joined_gu(f):
        part = part_f if f == 0 else part_b
        remote(xs_gu.at[f], xr_gu.at[f], dp_s.at[f], dp_r.at[f], partner).wait_recv()
        total = part[...] + xr_gu[f].astype(F32)
        return total[:, :FF], total[:, FF:]

    def back(f, hidden):
        hid[f, :, :, pl.ds(0, hidden.shape[-1])] = hidden.reshape(2, CHIPS * CAP, hidden.shape[-1])

    def product(f, core):
        if f == 0:
            return dot(hid[0, core, :, pl.ds(0, FF)], wd[...], ((1,), (0,)))
        return dot(hid[1, core], wgu[...], ((1,), (1,)))

    def to_sibling(f):
        sib_s[f] = product(f, 1 - c).astype(BF16).reshape(CHIPS, CAP, wd.shape[-1])
        send(sib_s.at[f], sib_r.at[f], ss_s.at[f], ss_r.at[f], sibling)
        own[f] = product(f, c).reshape(CHIPS, CAP, wd.shape[-1])

    def gathered(f, k):
        return own[f, chip(k)] + sib_r[f, chip(k)].astype(F32)

    def to_mate(f):
        remote(sib_s.at[f], sib_r.at[f], ss_s.at[f], ss_r.at[f], sibling).wait_recv()
        for k in STEPS + (0,):
            mate_s[f, k] = gathered(f, -1 - k).astype(BF16)
            send(mate_s.at[f, k], mate_r.at[f, k], ma_s.at[f, k], ma_r.at[f, k], at_chip(-1))

    def from_mate(f, k):
        remote(mate_s.at[f, k], mate_r.at[f, k], ma_s.at[f, k], ma_r.at[f, k], sibling).wait_recv()
        return (gathered(f, k) + mate_r[f, k].astype(F32)).astype(BF16)

    def combine(f):
        pair = lax.div(z, 2)
        for k in STEPS:
            com_s[f, k] = from_mate(f, k)
            send(com_s.at[f, k], com_r.at[f, pair], co_s.at[f, k], co_r.at[f, k], at_chip(k))
        com_r[f, pair] = from_mate(f, 0)

    def hand_on(f):
        for k in (1, 2, 3):
            source = lax.div(chip(goal[k]), 2)
            remote(com_s.at[f, k], com_r.at[f, source], co_s.at[f, k], co_r.at[f, k], sibling).wait_recv()
        for e in range(EXPERTS):
            total = com_r[f, 2 * e].astype(F32) + com_r[f, 2 * e + 1].astype(F32)
            if f == 0:
                total = weights[0][e] * total
            pip_s[f, e] = total.astype(BF16)
        send(pip_s.at[f], pip_r.at[f], pi_s.at[f], pi_r.at[f], after if f == 0 else before)

    def place(f):
        remote(lst.at[f], nlst.at[f], li_s.at[f], li_r.at[f], after).wait_recv()
        remote(pip_s.at[f], pip_r.at[f], pi_s.at[f], pi_r.at[f], after).wait_recv()
        total = None
        for e in range(EXPERTS):
            spot = placer(nlst[f, pl.ds(e, 1), pl.ds(0, CAP)]).astype(BF16)
            term = dot(spot, pip_r[f, e], ((1,), (0,)))
            total = term if total is None else total + term
        placed[f] = total.astype(BF16)
        copy = pltpu.make_async_copy(placed.at[f], (out_f if f == 0 else out_b).at[0], store_sem.at[f])
        copy.start()
        return copy

    relay(0)
    relay(1)
    collect(0)
    exchange_gu(0)
    relay(2)
    collect(1)
    exchange_gu(1)
    gate, up = joined_gu(0)
    back(0, (gate * jax.nn.sigmoid(gate) * up).astype(BF16))
    to_sibling(0)
    collect(2)
    part_g[...] = dot(all_rows(2), wd[...], ((1,), (1,)))
    xs_g[...] = part_g[...].astype(BF16)
    send(xs_g, xr_g, dp_s.at[2], dp_r.at[2], partner)
    to_mate(0)
    gate, up = joined_gu(1)
    sg = jax.nn.sigmoid(gate)
    remote(xs_g, xr_g, dp_s.at[2], dp_r.at[2], partner).wait_recv()
    grad = part_g[...] + xr_g[...].astype(F32)
    grad_gate = (grad * up * sg * (1.0 + gate * (1.0 - sg))).astype(BF16)
    grad_up = (grad * gate * sg).astype(BF16)
    back(1, jnp.concatenate([grad_gate, grad_up], axis=1))
    to_sibling(1)
    combine(0)
    to_mate(1)
    hand_on(0)
    combine(1)
    first = place(0)
    hand_on(1)
    second = place(1)
    for copy in sent:
        copy.wait_send()
    first.wait()
    second.wait()


def per_device(forward_input, saved_input, output_grad, gate_proj, up_proj, down_proj, affinity, token_lists, slot_ids):
    width = forward_input.shape[-1]
    whole = pl.BlockSpec(memory_space=pltpu.HBM)
    blocks = 2 * CHIPS
    entries = blocks * CAP
    dma = pltpu.SemaphoreType.DMA
    return pl.pallas_call(
        kernel,
        out_shape=(jax.ShapeDtypeStruct((1, TOK, width), BF16),) * 2,
        in_specs=[whole] * 9,
        out_specs=(whole, whole),
        scratch_shapes=[
            pltpu.VMEM((2, 1, CHIPS, TOK), F32),
            pltpu.VMEM((2, 1, 1, EXPERTS, CAP), I32),
            pltpu.VMEM((2, 1, 1, EXPERTS, CAP), I32),
            pltpu.VMEM((3, TOK, width), BF16),
            pltpu.VMEM((width, 2 * FF), BF16),
            pltpu.VMEM((FF, width), BF16),
            pltpu.VMEM((3, EXPERTS, CAP, width), BF16),
            pltpu.VMEM((3, blocks, CAP, width), BF16),
            pltpu.VMEM((2, 8, 128), I32),
            pltpu.VMEM((2, 8, 128), I32),
            pltpu.VMEM((entries, 2 * FF), F32),
            pltpu.VMEM((entries, 2 * FF), F32),
            pltpu.VMEM((entries, FF), F32),
            pltpu.VMEM((2, entries, 2 * FF), BF16),
            pltpu.VMEM((2, entries, 2 * FF), BF16),
            pltpu.VMEM((entries, FF), BF16),
            pltpu.VMEM((entries, FF), BF16),
            pltpu.VMEM((2, 2, CHIPS * CAP, 2 * FF), BF16),
            pltpu.VMEM((2, CHIPS, CAP, width), BF16),
            pltpu.VMEM((2, CHIPS, CAP, width), BF16),
            pltpu.VMEM((2, CHIPS, CAP, width), F32),
            pltpu.VMEM((2, 4, CAP, width), BF16),
            pltpu.VMEM((2, 4, CAP, width), BF16),
            pltpu.VMEM((2, 4, CAP, width), BF16),
            pltpu.VMEM((2, 4, CAP, width), BF16),
            pltpu.VMEM((2, EXPERTS, CAP, width), BF16),
            pltpu.VMEM((2, EXPERTS, CAP, width), BF16),
            pltpu.VMEM((2, TOK, width), BF16),
            dma((9,)), dma((2,)),
            dma((3, CHIPS)), dma((3, CHIPS)), dma((3, CHIPS)), dma((3, CHIPS)),
            dma((3,)), dma((3,)), dma((2,)), dma((2,)), dma((2, 4)), dma((2, 4)),
            dma((2, 4)), dma((2, 4)), dma((2,)), dma((2,)), dma((2,)), dma((2,)),
        ],
        compiler_params=pltpu.CompilerParams(
            collective_id=0, has_side_effects=True, vmem_limit_bytes=VMEM_LIMIT
        ),
        cost_estimate=pl.CostEstimate(flops=2_000_000_000, bytes_accessed=6_000_000, transcendentals=262_144),
    )(
        forward_input, saved_input, output_grad, gate_proj, up_proj, down_proj,
        jnp.swapaxes(affinity, 2, 3), token_lists, slot_ids,
    )


def solution(mesh):
    in_specs = (
        P("pipe", "expert", "dp"),
        P("pipe", "expert", "dp"),
        P("pipe", "expert", "dp"),
        P("pipe", "dp", "expert"),
        P("pipe", "dp", "expert"),
        P("pipe", "expert", "dp"),
        P(None, "pipe", "expert", None),
        P(None, "pipe", "expert", None, None),
        P(None, "pipe", "expert", None, None),
    )
    out_specs = (P("pipe", "expert", "dp"), P("pipe", "expert", "dp"))
    return jax.shard_map(
        per_device, mesh=mesh, in_specs=in_specs, out_specs=out_specs, check_vma=False
    )
```

```python
import functools

import jax
import jax.numpy as jnp
from jax import lax
from jax.experimental import pallas as pl
from jax.experimental.pallas import tpu as pltpu
from jax.sharding import PartitionSpec as P

MESH = pl.DeviceIdType.MESH
F32, BF16, I32 = jnp.float32, jnp.bfloat16, jnp.int32
ROUTED_SCALE = 2.5
EXPERTS = 2
CAP = 16
TOK = 128
CHIPS = 8
HALF = 4
FF = 256
VMEM_LIMIT = 62 * 1024 * 1024
STEPS = (3, 2, 1)
PEERS = (1, 2, 3, 4, -1, -2, -3)
EARLY = 5
SHARES = ((5, 8), (0, 5))
PARTS = ((0, EARLY), (EARLY, CHIPS))
CUTS = (((0, 1792),), ((0, 1792),))
MOST = 2


def dot(a, b, dims, precision=None):
    return lax.dot_general(a, b, ((dims[0], dims[1]), ((), ())), precision=precision, preferred_element_type=F32)


def column(row):
    wide = jnp.broadcast_to(row.astype(F32), (CAP, CAP))
    eye = lax.broadcasted_iota(I32, (CAP, CAP), 0) == lax.broadcasted_iota(I32, (CAP, CAP), 1)
    return jnp.sum(jnp.where(eye, wide, 0.0), axis=1, keepdims=True)


def picker(row):
    lanes = lax.broadcasted_iota(I32, (CAP, TOK), 1).astype(F32)
    return jnp.where(lanes == column(row), 1.0, 0.0)


def placer(row):
    tokens = lax.broadcasted_iota(I32, (TOK, CAP), 0)
    return jnp.where(tokens == jnp.broadcast_to(row, (TOK, CAP)), 1.0, 0.0)


def entry_weight(onehot, slot_row, affinity):
    picked = dot(onehot, affinity, ((1,), (1,)), lax.Precision.HIGHEST)
    slots = lax.broadcasted_iota(I32, (CAP, CHIPS), 1).astype(F32)
    chosen = jnp.sum(jnp.where(slots == column(slot_row), picked, 0.0), axis=1, keepdims=True)
    total = jnp.sum(picked, axis=1, keepdims=True)
    live = total > 0.0
    return jnp.where(live, ROUTED_SCALE * (chosen / jnp.where(live, total, 1.0)), 0.0)


def spread(rows_h, spots_h, out_f, out_b, rows, spots, placed, load_sem, store_sem):
    loads = [
        pltpu.make_async_copy(spots_h, spots, load_sem.at[0]),
        pltpu.make_async_copy(rows_h.at[0], rows.at[0], load_sem.at[1]),
        pltpu.make_async_copy(rows_h.at[1], rows.at[1], load_sem.at[2]),
    ]
    for load in loads:
        load.start()
    loads[0].wait()
    stores = []
    for f, out in enumerate((out_f, out_b)):
        loads[1 + f].wait()
        total = None
        for e in range(EXPERTS):
            spot = placer(spots[f, pl.ds(e, 1), pl.ds(0, CAP)]).astype(BF16)
            term = dot(spot, rows[f, e], ((1,), (0,)))
            total = term if total is None else total + term
        placed[f] = total.astype(BF16)
        stores.append(pltpu.make_async_copy(placed.at[f], out.at[0], store_sem.at[f]))
        stores[f].start()
    for store in stores:
        store.wait()


def kernel(
    fin, sav, gra, wg_h, wu_h, wd_h, aff_h, lists_h, slots_h,
    out_p, out_l,
    aff, lists, slots, vx, wgu, wd, snd, rcv, lst, nlst,
    part_f, part_b, part_g, xs_gu, xr_gu, xs_g, xr_g,
    hid, sib_s, sib_r, own, mate_s, mate_r, com_s, com_r, pip_s, pip_r,
    load_sem, store_sem, dis_s, dis_r, fwd_s, fwd_r, dp_s, dp_r, ss_s, ss_r, ma_s, ma_r, co_s, co_r, pi_s, pi_r, li_s, li_r,
):
    p, x, d = lax.axis_index("pipe"), lax.axis_index("expert"), lax.axis_index("dp")
    pipes = lax.axis_size("pipe")
    z, c = lax.div(x, 2), lax.rem(x, 2)
    half = lax.div(z, HALF)
    sibling = (p, z * 2 + 1 - c, d)
    partner = (p, x, 1 - d)
    after = (lax.rem(p + 1, pipes), x, d)
    before = (lax.rem(p + pipes - 1, pipes), x, d)
    toward = 2 * lax.rem(z, 2) - 1
    chip = lambda k: lax.rem(z + CHIPS + k * toward, CHIPS)
    at_chip = lambda k: (p, chip(k) * 2 + c, d)
    goal = {1: 1, 2: -2, 3: 3}
    sent = []

    barrier = pltpu.get_barrier_semaphore()
    for peer in [at_chip(k) for k in PEERS] + [sibling, partner, after, before]:
        pl.semaphore_signal(barrier, inc=1, device_id=peer, device_id_type=MESH)

    loads = [
        pltpu.make_async_copy(src, dst, load_sem.at[i])
        for i, (src, dst) in enumerate([
            (fin.at[0], vx.at[0]), (sav.at[0], vx.at[1]), (gra.at[0], vx.at[2]),
            (wg_h.at[0], wgu.at[:, pl.ds(0, FF)]), (wu_h.at[0], wgu.at[:, pl.ds(FF, FF)]), (wd_h.at[0], wd),
            (lists_h, lists), (slots_h, slots), (aff_h, aff),
        ])
    ]
    for i in (6, 0, 1, 2, 7, 8, 3, 4, 5):
        loads[i].start()

    def remote(src, dst, send_sem, recv_sem, device):
        return pltpu.make_async_remote_copy(
            src_ref=src, dst_ref=dst, send_sem=send_sem, recv_sem=recv_sem, device_id=device, device_id_type=MESH
        )

    def send(*args):
        copy = remote(*args)
        copy.start()
        sent.append(copy)

    def pick(f):
        return [picker(lists[f, 0, 0, pl.ds(e, 1), :]) for e in range(EXPERTS)]

    def weigh(f, picks):
        return [entry_weight(picks[e], slots[f, 0, 0, pl.ds(e, 1), :], aff[f, 0]) for e in range(EXPERTS)]

    def gather(a, picks, weights=None):
        got = dot(jnp.concatenate(picks, axis=0).astype(BF16), vx[a], ((1,), (0,)))
        for e in range(EXPERTS):
            block = got[e * CAP : (e + 1) * CAP]
            if weights is not None:
                block = weights[e] * block
            snd[a, e] = block.astype(BF16)
        rcv[a, 0, 0] = snd[a, half]

    def dispatch(a):
        for k in STEPS:
            send(
                snd.at[a, lax.div(chip(goal[k]), HALF)], rcv.at[a, 0, k],
                dis_s.at[a, k], dis_r.at[a, k], at_chip(goal[k]),
            )
        send(snd.at[a, half], rcv.at[a, 0, 4], dis_s.at[a, 4], dis_r.at[a, 4], at_chip(-1))
        share(a, 0)

    def share(a, i):
        send(rcv.at[a, 0, i], rcv.at[a, 1, i], fwd_s.at[a, i], fwd_r.at[a, i], sibling)

    def arrived(a, i):
        remote(snd.at[a, 0], rcv.at[a, 0, i], dis_s.at[a, i], dis_r.at[a, i], sibling).wait_recv()

    def shared(a, first, last):
        for i in range(first, last):
            remote(snd.at[a, 0], rcv.at[a, 1, i], fwd_s.at[a, i], fwd_r.at[a, i], sibling).wait_recv()

    def relay(a):
        for k in (1, 2, 3):
            arrived(a, k)
            send(rcv.at[a, 0, k], rcv.at[a, 0, 4 + k], dis_s.at[a, 4 + k], dis_r.at[a, 4 + k], at_chip(-1))
            share(a, k)

    def collect_early(a):
        arrived(a, 4)
        share(a, 4)
        shared(a, 0, EARLY)

    def collect_late(a):
        for i in range(EARLY, CHIPS):
            arrived(a, i)
            share(a, i)
        shared(a, EARLY, CHIPS)

    def collect(a):
        arrived(a, 4)
        share(a, 4)
        collect_late(a)
        shared(a, 0, EARLY)

    def all_rows(a):
        return rcv[a].reshape(2 * CHIPS * CAP, rcv.shape[-1])

    loads[6].wait()
    picks = [pick(0)]
    loads[0].wait()
    gather(0, picks[0])
    pl.semaphore_wait(barrier, len(PEERS) + 4)
    dispatch(0)
    picks.append(pick(1))
    loads[1].wait()
    gather(1, picks[1])
    dispatch(1)
    loads[7].wait()
    loads[8].wait()
    loads[2].wait()
    gather(2, picks[1], weigh(1, picks[1]))
    lst[...] = jnp.zeros_like(lst)
    for f in range(2):
        lst[f, pl.ds(0, EXPERTS), pl.ds(0, CAP)] = lists[f, 0, 0]
    send(lst.at[0], nlst.at[0], li_s.at[0], li_r.at[0], after)
    send(lst.at[1], nlst.at[1], li_s.at[1], li_r.at[1], before)
    weights = weigh(0, picks[0])
    for load in loads[3:6]:
        load.wait()

    def exchange_gu(f, i=0, first=0, last=CHIPS):
        part = part_f if f == 0 else part_b
        rows = (last - first) * CAP
        at = pl.ds(first * CAP, rows)
        got = dot(rcv[f, :, pl.ds(first, last - first)].reshape(2 * rows, wd.shape[-1]), wgu[...], ((1,), (0,)))
        got = got.reshape(2, rows, 2 * FF)
        part[:, at, :] = got
        xs_gu[f, :, at, :] = got.astype(BF16)
        send(xs_gu.at[f, :, at], xr_gu.at[f, :, at], dp_s.at[f, i], dp_r.at[f, i], partner)

    def joined_gu(f, parts=((0, CHIPS),)):
        part = part_f if f == 0 else part_b
        for i, (first, last) in enumerate(parts):
            at = pl.ds(first * CAP, (last - first) * CAP)
            remote(xs_gu.at[f, :, at], xr_gu.at[f, :, at], dp_s.at[f, i], dp_r.at[f, i], partner).wait_recv()
        total = (part[...] + xr_gu[f].astype(F32)).reshape(2 * CHIPS * CAP, 2 * FF)
        return total[:, :FF], total[:, FF:]

    def product(f):
        for j, (at, width) in enumerate(CUTS[f]):
            cols = pl.ds(at, width)
            if f == 0:
                got = dot(hid[0, :, pl.ds(0, FF)], wd[:, cols], ((1,), (0,)))
            else:
                got = dot(hid[1], wgu[cols, :], ((1,), (1,)))
            got = got.reshape(2, CHIPS, CAP, width)
            sib_s[f, :, :, cols] = got[1].astype(BF16)
            for i, (first, last) in enumerate(SHARES):
                at = pl.ds(first, last - first)
                send(sib_s.at[f, at, :, cols], sib_r.at[f, at, :, cols], ss_s.at[f, j, i], ss_r.at[f, j, i], sibling)
            own[f, :, :, cols] = got[0]

    def gathered(f, i, cols):
        return own[f, i, :, cols] + sib_r[f, i, :, cols].astype(F32)

    def shared_sum(f, j, i):
        cols = pl.ds(*CUTS[f][j])
        first, last = SHARES[i]
        at = pl.ds(first, last - first)
        remote(
            sib_s.at[f, at, :, cols], sib_r.at[f, at, :, cols], ss_s.at[f, j, i], ss_r.at[f, j, i], sibling
        ).wait_recv()

    def to_mate(f, j):
        cols = pl.ds(*CUTS[f][j])
        for i, (first, last) in enumerate(SHARES[:1]):
            shared_sum(f, j, i)
        for k in STEPS:
            mate_s[f, k, :, cols] = gathered(f, 4 + k, cols).astype(BF16)
            send(mate_s.at[f, k, :, cols], mate_r.at[f, k, :, cols], ma_s.at[f, j, k], ma_r.at[f, j, k], at_chip(-1))

    def mate_own(f, j):
        cols = pl.ds(*CUTS[f][j])
        mate_s[f, 0, :, cols] = gathered(f, 4, cols).astype(BF16)
        send(mate_s.at[f, 0, :, cols], mate_r.at[f, 0, :, cols], ma_s.at[f, j, 0], ma_r.at[f, j, 0], at_chip(-1))

    def from_mate(f, j, k):
        cols = pl.ds(*CUTS[f][j])
        remote(mate_s.at[f, k, :, cols], mate_r.at[f, k, :, cols], ma_s.at[f, j, k], ma_r.at[f, j, k], sibling).wait_recv()
        return (gathered(f, k, cols) + mate_r[f, k, :, cols].astype(F32)).astype(BF16)

    def combine(f, j):
        cols = pl.ds(*CUTS[f][j])
        pair = lax.div(z, 2)
        shared_sum(f, j, 1)
        for k in STEPS:
            com_s[f, k, :, cols] = from_mate(f, j, k)
            send(com_s.at[f, k, :, cols], com_r.at[f, pair, :, cols], co_s.at[f, j, k], co_r.at[f, j, k], at_chip(k))
            if k == STEPS[0]:
                mate_own(f, j)
        com_r[f, pair, :, cols] = from_mate(f, j, 0)

    def hand_on(f, j):
        cols = pl.ds(*CUTS[f][j])
        for k in (1, 2, 3):
            source = lax.div(chip(goal[k]), 2)
            remote(
                com_s.at[f, k, :, cols], com_r.at[f, source, :, cols], co_s.at[f, j, k], co_r.at[f, j, k], sibling
            ).wait_recv()
        for e in range(EXPERTS):
            total = com_r[f, 2 * e, :, cols].astype(F32) + com_r[f, 2 * e + 1, :, cols].astype(F32)
            if f == 0:
                total = weights[e] * total
            pip_s[f, e, :, cols] = total.astype(BF16)
        send(
            pip_s.at[f, :, :, cols], pip_r.at[f, :, :, cols], pi_s.at[f, j], pi_r.at[f, j], after if f == 0 else before
        )

    stores = []

    def place(f, j):
        cols = pl.ds(*CUTS[f][j])
        if j == 0:
            remote(lst.at[f], nlst.at[f], li_s.at[f], li_r.at[f], after).wait_recv()
            copy = pltpu.make_async_copy(nlst.at[f], out_l.at[f], store_sem.at[f, 0])
            copy.start()
            stores.append(copy)
        remote(pip_s.at[f, :, :, cols], pip_r.at[f, :, :, cols], pi_s.at[f, j], pi_r.at[f, j], after).wait_recv()
        copy = pltpu.make_async_copy(pip_r.at[f, :, :, cols], out_p.at[f, :, :, cols], store_sem.at[f, 1 + j])
        copy.start()
        stores.append(copy)

    def exchange_grad(i, first, last):
        rows = (last - first) * CAP
        got = dot(rcv[2, :, pl.ds(first, last - first)].reshape(2 * rows, wd.shape[-1]), wd[...], ((1,), (1,)))
        got = got.reshape(2, rows, FF)
        at = pl.ds(first * CAP, rows)
        part_g[:, at, :] = got
        xs_g[:, at, :] = got.astype(BF16)
        send(xs_g.at[:, at], xr_g.at[:, at], dp_s.at[2, i], dp_r.at[2, i], partner)

    def joined_grad(i, first, last):
        at = pl.ds(first * CAP, (last - first) * CAP)
        remote(xs_g.at[:, at], xr_g.at[:, at], dp_s.at[2, i], dp_r.at[2, i], partner).wait_recv()

    relay(0)
    relay(1)
    dispatch(2)
    collect_early(0)
    exchange_gu(0, 0, *PARTS[0])
    collect_late(0)
    exchange_gu(0, 1, *PARTS[1])
    collect_early(1)
    exchange_gu(1, 0, *PARTS[0])
    relay(2)
    collect_late(1)
    exchange_gu(1, 1, *PARTS[1])
    gate, up = joined_gu(0, PARTS)
    hid[0, :, pl.ds(0, FF)] = (gate * jax.nn.sigmoid(gate) * up).astype(BF16)
    product(0)
    collect_early(2)
    exchange_grad(0, *PARTS[0])
    to_mate(0, 0)
    collect_late(2)
    exchange_grad(1, *PARTS[1])
    gate, up = joined_gu(1, PARTS)
    sg = jax.nn.sigmoid(gate)
    by_gate = up * sg * (1.0 + gate * (1.0 - sg))
    by_up = gate * sg
    combine(0, 0)
    joined_grad(0, *PARTS[0])
    joined_grad(1, *PARTS[1])
    grad = (part_g[...] + xr_g[...].astype(F32)).reshape(2 * CHIPS * CAP, FF)
    hid[1, :, pl.ds(0, FF)] = (grad * by_gate).astype(BF16)
    hid[1, :, pl.ds(FF, FF)] = (grad * by_up).astype(BF16)
    product(1)
    to_mate(1, 0)
    hand_on(0, 0)
    combine(1, 0)
    place(0, 0)
    hand_on(1, 0)
    place(1, 0)
    for copy in sent:
        copy.wait_send()
    for copy in stores:
        copy.wait()


def per_device(forward_input, saved_input, output_grad, gate_proj, up_proj, down_proj, affinity, token_lists, slot_ids):
    width = forward_input.shape[-1]
    whole = pl.BlockSpec(memory_space=pltpu.HBM)
    blocks = 2 * CHIPS
    entries = blocks * CAP
    dma = pltpu.SemaphoreType.DMA
    rows, spots = pl.pallas_call(
        kernel,
        out_shape=(
            jax.ShapeDtypeStruct((2, EXPERTS, CAP, width), BF16),
            jax.ShapeDtypeStruct((2, 8, TOK), I32),
        ),
        in_specs=[whole] * 9,
        out_specs=(whole, whole),
        scratch_shapes=[
            pltpu.VMEM((2, 1, CHIPS, TOK), F32),
            pltpu.VMEM((2, 1, 1, EXPERTS, CAP), I32),
            pltpu.VMEM((2, 1, 1, EXPERTS, CAP), I32),
            pltpu.VMEM((3, TOK, width), BF16),
            pltpu.VMEM((width, 2 * FF), BF16),
            pltpu.VMEM((FF, width), BF16),
            pltpu.VMEM((3, EXPERTS, CAP, width), BF16),
            pltpu.VMEM((3, 2, CHIPS, CAP, width), BF16),
            pltpu.VMEM((2, 8, 128), I32),
            pltpu.VMEM((2, 8, 128), I32),
            pltpu.VMEM((2, CHIPS * CAP, 2 * FF), F32),
            pltpu.VMEM((2, CHIPS * CAP, 2 * FF), F32),
            pltpu.VMEM((2, CHIPS * CAP, FF), F32),
            pltpu.VMEM((2, 2, CHIPS * CAP, 2 * FF), BF16),
            pltpu.VMEM((2, 2, CHIPS * CAP, 2 * FF), BF16),
            pltpu.VMEM((2, CHIPS * CAP, FF), BF16),
            pltpu.VMEM((2, CHIPS * CAP, FF), BF16),
            pltpu.VMEM((2, entries, 2 * FF), BF16),
            pltpu.VMEM((2, CHIPS, CAP, width), BF16),
            pltpu.VMEM((2, CHIPS, CAP, width), BF16),
            pltpu.VMEM((2, CHIPS, CAP, width), F32),
            pltpu.VMEM((2, 4, CAP, width), BF16),
            pltpu.VMEM((2, 4, CAP, width), BF16),
            pltpu.VMEM((2, 4, CAP, width), BF16),
            pltpu.VMEM((2, 4, CAP, width), BF16),
            pltpu.VMEM((2, EXPERTS, CAP, width), BF16),
            pltpu.VMEM((2, EXPERTS, CAP, width), BF16),
            dma((9,)), dma((2, 1 + MOST)),
            dma((3, CHIPS)), dma((3, CHIPS)), dma((3, CHIPS)), dma((3, CHIPS)),
            dma((3, 2)), dma((3, 2)), dma((2, MOST, 2)), dma((2, MOST, 2)), dma((2, MOST, 4)), dma((2, MOST, 4)),
            dma((2, MOST, 4)), dma((2, MOST, 4)), dma((2, MOST)), dma((2, MOST)), dma((2,)), dma((2,)),
        ],
        compiler_params=pltpu.CompilerParams(
            collective_id=0, has_side_effects=True, vmem_limit_bytes=VMEM_LIMIT
        ),
        cost_estimate=pl.CostEstimate(flops=2_000_000_000, bytes_accessed=6_000_000, transcendentals=262_144),
    )(
        forward_input, saved_input, output_grad, gate_proj, up_proj, down_proj,
        jnp.swapaxes(affinity, 2, 3), token_lists, slot_ids,
    )
    return pl.pallas_call(
        spread,
        out_shape=(jax.ShapeDtypeStruct((1, TOK, width), BF16),) * 2,
        in_specs=[whole] * 2,
        out_specs=(whole, whole),
        scratch_shapes=[
            pltpu.VMEM((2, EXPERTS, CAP, width), BF16),
            pltpu.VMEM((2, 8, TOK), I32),
            pltpu.VMEM((2, TOK, width), BF16),
            dma((3,)), dma((2,)),
        ],
        compiler_params=pltpu.CompilerParams(vmem_limit_bytes=VMEM_LIMIT),
    )(rows, spots)


def solution(mesh):
    in_specs = (
        P("pipe", "expert", "dp"),
        P("pipe", "expert", "dp"),
        P("pipe", "expert", "dp"),
        P("pipe", "dp", "expert"),
        P("pipe", "dp", "expert"),
        P("pipe", "expert", "dp"),
        P(None, "pipe", "expert", None),
        P(None, "pipe", "expert", None, None),
        P(None, "pipe", "expert", None, None),
    )
    out_specs = (P("pipe", "expert", "dp"), P("pipe", "expert", "dp"))
    return jax.shard_map(
        per_device, mesh=mesh, in_specs=in_specs, out_specs=out_specs, check_vma=False
    )
```

```python
import functools

import jax
import jax.numpy as jnp
from jax import lax
from jax.experimental import pallas as pl
from jax.experimental.pallas import tpu as pltpu
from jax.sharding import PartitionSpec as P

MESH = pl.DeviceIdType.MESH
F32, BF16, I32 = jnp.float32, jnp.bfloat16, jnp.int32
ROUTED_SCALE = 2.5
EXPERTS = 2
CAP = 16
TOK = 128
CHIPS = 8
HALF = 4
FF = 256
VMEM_LIMIT = 62 * 1024 * 1024
STEPS = (3, 2, 1)
PEERS = (1, 2, 3, -1, -2)
BEYOND = (0, 1, 2, 3, -2)
MIRROR = {0: 0, 1: 1, 2: -2, 3: 3, -2: 2}
EARLY = 5
SHARES = ((5, 8), (0, 5))
PARTS = ((0, EARLY), (EARLY, CHIPS))
CUTS = (((0, 1792),), ((0, 1792),))
MOST = 2


def dot(a, b, dims, precision=None):
    return lax.dot_general(a, b, ((dims[0], dims[1]), ((), ())), precision=precision, preferred_element_type=F32)


def column(row):
    wide = jnp.broadcast_to(row.astype(F32), (CAP, CAP))
    eye = lax.broadcasted_iota(I32, (CAP, CAP), 0) == lax.broadcasted_iota(I32, (CAP, CAP), 1)
    return jnp.sum(jnp.where(eye, wide, 0.0), axis=1, keepdims=True)


def picker(row):
    lanes = lax.broadcasted_iota(I32, (CAP, TOK), 1).astype(F32)
    return jnp.where(lanes == column(row), 1.0, 0.0)


def placer(row):
    tokens = lax.broadcasted_iota(I32, (TOK, CAP), 0)
    return jnp.where(tokens == jnp.broadcast_to(row, (TOK, CAP)), 1.0, 0.0)


def entry_weight(onehot, slot_row, affinity):
    picked = dot(onehot, affinity, ((1,), (1,)), lax.Precision.HIGHEST)
    slots = lax.broadcasted_iota(I32, (CAP, CHIPS), 1).astype(F32)
    chosen = jnp.sum(jnp.where(slots == column(slot_row), picked, 0.0), axis=1, keepdims=True)
    total = jnp.sum(picked, axis=1, keepdims=True)
    live = total > 0.0
    return jnp.where(live, ROUTED_SCALE * (chosen / jnp.where(live, total, 1.0)), 0.0)


def spread(rows_h, spots_h, out_f, out_b, rows, spots, placed, load_sem, store_sem):
    loads = [
        pltpu.make_async_copy(spots_h, spots, load_sem.at[0]),
        pltpu.make_async_copy(rows_h.at[0], rows.at[0], load_sem.at[1]),
        pltpu.make_async_copy(rows_h.at[1], rows.at[1], load_sem.at[2]),
    ]
    for load in loads:
        load.start()
    loads[0].wait()
    stores = []
    for f, out in enumerate((out_f, out_b)):
        loads[1 + f].wait()
        total = None
        for e in range(EXPERTS):
            spot = placer(spots[f, pl.ds(e, 1), pl.ds(0, CAP)]).astype(BF16)
            term = dot(spot, rows[f, e], ((1,), (0,)))
            total = term if total is None else total + term
        placed[f] = total.astype(BF16)
        stores.append(pltpu.make_async_copy(placed.at[f], out.at[0], store_sem.at[f]))
        stores[f].start()
    for store in stores:
        store.wait()


def kernel(
    fin, sav, gra, wg_h, wu_h, wd_h, aff_h, lists_h, slots_h,
    out_p, out_l,
    aff, lists, slots, vx, wgu, wd, snd, rcv, lst, nlst, wei, nwei,
    part_f, part_b, part_g, xs_gu, xr_gu, xs_g, xr_g,
    hid, sib_s, sib_r, own, mate_s, mate_r, com_s, com_r, ended,
    load_sem, store_sem, dis_s, dis_r, fwd_s, fwd_r, dp_s, dp_r, ss_s, ss_r, ma_s, ma_r, co_s, co_r, li_s, li_r, ready,
):
    p, x, d = lax.axis_index("pipe"), lax.axis_index("expert"), lax.axis_index("dp")
    pipes = lax.axis_size("pipe")
    z, c = lax.div(x, 2), lax.rem(x, 2)
    half = lax.div(z, HALF)
    sibling = (p, z * 2 + 1 - c, d)
    partner = (p, x, 1 - d)
    after = (lax.rem(p + 1, pipes), x, d)
    before = (lax.rem(p + pipes - 1, pipes), x, d)
    toward = 2 * lax.rem(z, 2) - 1
    chip = lambda k: lax.rem(z + CHIPS + k * toward, CHIPS)
    at_chip = lambda k: (p, chip(k) * 2 + c, d)
    goal = {0: 0, 1: 1, 2: -2, 3: 3}
    far = lambda f, k: ((after, before)[f][0], chip(k) * 2 + c, d)
    sent = []

    beyond = [(f, k) for f in range(2) for k in BEYOND]
    higher = (after[0] > p, before[0] > p)

    barrier = pltpu.get_barrier_semaphore()
    for peer in [sibling, partner] + [at_chip(k) for k in PEERS]:
        pl.semaphore_signal(barrier, inc=1, device_id=peer, device_id_type=MESH)
    for f, k in beyond:

        @pl.when(higher[f])
        def _(f=f, k=k):
            pl.semaphore_signal(barrier, inc=1, device_id=far(f, k), device_id_type=MESH)

    def enter():
        lower = 2 - higher[0].astype(I32) - higher[1].astype(I32)
        pl.semaphore_wait(barrier, len(PEERS) + 2 + len(BEYOND) * lower)
        for f, k in beyond:

            @pl.when(jnp.logical_not(higher[f]))
            def _(f=f, k=k):
                i = beyond.index((1 - f, MIRROR[k]))
                pl.semaphore_signal(ready.at[i], inc=1, device_id=far(f, k), device_id_type=MESH)

    def until_ready(f, k):
        @pl.when(higher[f])
        def _():
            pl.semaphore_wait(ready.at[beyond.index((f, k))], 1)

    loads = [
        pltpu.make_async_copy(src, dst, load_sem.at[i])
        for i, (src, dst) in enumerate([
            (fin.at[0], vx.at[0]), (sav.at[0], vx.at[1]), (gra.at[0], vx.at[2]),
            (wg_h.at[0], wgu.at[:, pl.ds(0, FF)]), (wu_h.at[0], wgu.at[:, pl.ds(FF, FF)]), (wd_h.at[0], wd),
            (lists_h, lists), (slots_h, slots), (aff_h, aff),
        ])
    ]
    for i in (6, 0, 1, 7, 8, 2):
        loads[i].start()

    def remote(src, dst, send_sem, recv_sem, device):
        return pltpu.make_async_remote_copy(
            src_ref=src, dst_ref=dst, send_sem=send_sem, recv_sem=recv_sem, device_id=device, device_id_type=MESH
        )

    def send(*args):
        copy = remote(*args)
        copy.start()
        sent.append(copy)

    def pick(f):
        return [picker(lists[f, 0, 0, pl.ds(e, 1), :]) for e in range(EXPERTS)]

    def weigh(f, picks):
        return [entry_weight(picks[e], slots[f, 0, 0, pl.ds(e, 1), :], aff[f, 0]) for e in range(EXPERTS)]

    def gather(a, picks, weights=None):
        got = dot(jnp.concatenate(picks, axis=0).astype(BF16), vx[a], ((1,), (0,)))
        for e in range(EXPERTS):
            block = got[e * CAP : (e + 1) * CAP]
            if weights is not None:
                block = weights[e] * block
            snd[a, e] = block.astype(BF16)
        rcv[a, 0, 0] = snd[a, half]

    def dispatch(a):
        for k in STEPS:
            send(
                snd.at[a, lax.div(chip(goal[k]), HALF)], rcv.at[a, 0, k],
                dis_s.at[a, k], dis_r.at[a, k], at_chip(goal[k]),
            )
        send(snd.at[a, half], rcv.at[a, 0, 4], dis_s.at[a, 4], dis_r.at[a, 4], at_chip(-1))
        share(a, 0)

    def share(a, i):
        send(rcv.at[a, 0, i], rcv.at[a, 1, i], fwd_s.at[a, i], fwd_r.at[a, i], sibling)

    def arrived(a, i):
        remote(snd.at[a, 0], rcv.at[a, 0, i], dis_s.at[a, i], dis_r.at[a, i], sibling).wait_recv()

    def shared(a, first, last):
        for i in range(first, last):
            remote(snd.at[a, 0], rcv.at[a, 1, i], fwd_s.at[a, i], fwd_r.at[a, i], sibling).wait_recv()

    def relay(a):
        for k in (1, 2, 3):
            arrived(a, k)
            send(rcv.at[a, 0, k], rcv.at[a, 0, 4 + k], dis_s.at[a, 4 + k], dis_r.at[a, 4 + k], at_chip(-1))
            share(a, k)

    def collect_early(a):
        arrived(a, 4)
        share(a, 4)
        shared(a, 0, EARLY)

    def collect_late(a):
        for i in range(EARLY, CHIPS):
            arrived(a, i)
            share(a, i)
        shared(a, EARLY, CHIPS)

    def collect(a):
        arrived(a, 4)
        share(a, 4)
        collect_late(a)
        shared(a, 0, EARLY)

    def all_rows(a):
        return rcv[a].reshape(2 * CHIPS * CAP, rcv.shape[-1])

    loads[6].wait()
    picks = [pick(0)]
    loads[0].wait()
    gather(0, picks[0])
    enter()
    dispatch(0)
    for i in (3, 4, 5):
        loads[i].start()
    picks.append(pick(1))
    loads[1].wait()
    gather(1, picks[1])
    dispatch(1)
    loads[7].wait()
    loads[8].wait()
    loads[2].wait()
    gather(2, picks[1], weigh(1, picks[1]))
    lst[...] = jnp.zeros_like(lst)
    for f in range(2):
        lst[f, pl.ds(0, EXPERTS), pl.ds(0, CAP)] = lists[f, 0, 0]
    weights = weigh(0, picks[0])
    for e in range(EXPERTS):
        wei[e] = jnp.broadcast_to(weights[e], (CAP, TOK))
    for load in loads[3:6]:
        load.wait()

    def exchange_gu(f, i=0, first=0, last=CHIPS):
        part = part_f if f == 0 else part_b
        rows = (last - first) * CAP
        at = pl.ds(first * CAP, rows)
        got = dot(rcv[f, :, pl.ds(first, last - first)].reshape(2 * rows, wd.shape[-1]), wgu[...], ((1,), (0,)))
        got = got.reshape(2, rows, 2 * FF)
        part[:, at, :] = got
        xs_gu[f, :, at, :] = got.astype(BF16)
        send(xs_gu.at[f, :, at], xr_gu.at[f, :, at], dp_s.at[f, i], dp_r.at[f, i], partner)

    def joined_gu(f, parts=((0, CHIPS),)):
        part = part_f if f == 0 else part_b
        for i, (first, last) in enumerate(parts):
            at = pl.ds(first * CAP, (last - first) * CAP)
            remote(xs_gu.at[f, :, at], xr_gu.at[f, :, at], dp_s.at[f, i], dp_r.at[f, i], partner).wait_recv()
        total = (part[...] + xr_gu[f].astype(F32)).reshape(2 * CHIPS * CAP, 2 * FF)
        return total[:, :FF], total[:, FF:]

    def product(f):
        for j, (at, width) in enumerate(CUTS[f]):
            cols = pl.ds(at, width)
            if f == 0:
                got = dot(hid[0, :, pl.ds(0, FF)], wd[:, cols], ((1,), (0,)))
            else:
                got = dot(hid[1], wgu[cols, :], ((1,), (1,)))
            got = got.reshape(2, CHIPS, CAP, width)
            sib_s[f, :, :, cols] = got[1].astype(BF16)
            for i, (first, last) in enumerate(SHARES):
                at = pl.ds(first, last - first)
                send(sib_s.at[f, at, :, cols], sib_r.at[f, at, :, cols], ss_s.at[f, j, i], ss_r.at[f, j, i], sibling)
            own[f, :, :, cols] = got[0]

    def gathered(f, i, cols):
        return own[f, i, :, cols] + sib_r[f, i, :, cols].astype(F32)

    def shared_sum(f, j, i):
        cols = pl.ds(*CUTS[f][j])
        first, last = SHARES[i]
        at = pl.ds(first, last - first)
        remote(
            sib_s.at[f, at, :, cols], sib_r.at[f, at, :, cols], ss_s.at[f, j, i], ss_r.at[f, j, i], sibling
        ).wait_recv()

    def to_mate(f, j):
        cols = pl.ds(*CUTS[f][j])
        for i, (first, last) in enumerate(SHARES[:1]):
            shared_sum(f, j, i)
        for k in STEPS:
            mate_s[f, k, :, cols] = gathered(f, 4 + k, cols).astype(BF16)
            send(mate_s.at[f, k, :, cols], mate_r.at[f, k, :, cols], ma_s.at[f, j, k], ma_r.at[f, j, k], at_chip(-1))

    def mate_own(f, j):
        cols = pl.ds(*CUTS[f][j])
        mate_s[f, 0, :, cols] = gathered(f, 4, cols).astype(BF16)
        send(mate_s.at[f, 0, :, cols], mate_r.at[f, 0, :, cols], ma_s.at[f, j, 0], ma_r.at[f, j, 0], at_chip(-1))

    def from_mate(f, j, k):
        cols = pl.ds(*CUTS[f][j])
        remote(mate_s.at[f, k, :, cols], mate_r.at[f, k, :, cols], ma_s.at[f, j, k], ma_r.at[f, j, k], sibling).wait_recv()
        return (gathered(f, k, cols) + mate_r[f, k, :, cols].astype(F32)).astype(BF16)

    def combine(f, j):
        cols = pl.ds(*CUTS[f][j])
        for k in (1, 2, 3):
            until_ready(f, k)
        pair = lax.div(z, 2)
        shared_sum(f, j, 1)
        for k in STEPS:
            com_s[f, k, :, cols] = from_mate(f, j, k)
            send(com_s.at[f, k, :, cols], com_r.at[f, pair, :, cols], co_s.at[f, j, k], co_r.at[f, j, k], far(f, k))
            if k == STEPS[0]:
                mate_own(f, j)
        com_s[f, 0, :, cols] = from_mate(f, j, 0)
        send(com_s.at[f, 0, :, cols], com_r.at[f, pair, :, cols], co_s.at[f, j, 0], co_r.at[f, j, 0], far(f, 0))

    stores = []

    def finish(f, j):
        cols = pl.ds(*CUTS[f][j])
        if j == 0:
            remote(lst.at[f], nlst.at[f], li_s.at[f], li_r.at[f], after).wait_recv()
            stores.append(pltpu.make_async_copy(nlst.at[f], out_l.at[f], store_sem.at[f, 0]))
            stores[-1].start()
            if f == 0:
                remote(wei, nwei, li_s.at[2], li_r.at[2], after).wait_recv()
        for k in (1, 2, 3, 0):
            source = lax.div(chip(goal[k]), 2)
            remote(
                com_s.at[f, k, :, cols], com_r.at[f, source, :, cols], co_s.at[f, j, k], co_r.at[f, j, k], sibling
            ).wait_recv()
        for e in range(EXPERTS):
            total = com_r[f, 2 * e, :, cols].astype(F32) + com_r[f, 2 * e + 1, :, cols].astype(F32)
            if f == 0:
                total = nwei[e, :, pl.ds(0, 1)] * total
            ended[f, e, :, cols] = total.astype(BF16)
        stores.append(pltpu.make_async_copy(ended.at[f, :, :, cols], out_p.at[f, :, :, cols], store_sem.at[f, 1 + j]))
        stores[-1].start()

    def exchange_grad(i, first, last):
        rows = (last - first) * CAP
        got = dot(rcv[2, :, pl.ds(first, last - first)].reshape(2 * rows, wd.shape[-1]), wd[...], ((1,), (1,)))
        got = got.reshape(2, rows, FF)
        at = pl.ds(first * CAP, rows)
        part_g[:, at, :] = got
        xs_g[:, at, :] = got.astype(BF16)
        send(xs_g.at[:, at], xr_g.at[:, at], dp_s.at[2, i], dp_r.at[2, i], partner)

    def joined_grad(i, first, last):
        at = pl.ds(first * CAP, (last - first) * CAP)
        remote(xs_g.at[:, at], xr_g.at[:, at], dp_s.at[2, i], dp_r.at[2, i], partner).wait_recv()

    relay(0)
    relay(1)
    dispatch(2)
    collect_early(0)
    exchange_gu(0, 0, *PARTS[0])
    collect_late(0)
    exchange_gu(0, 1, *PARTS[1])
    collect_early(1)
    exchange_gu(1, 0, *PARTS[0])
    relay(2)
    collect_late(1)
    exchange_gu(1, 1, *PARTS[1])
    for f in range(2):
        until_ready(f, 0)
    send(lst.at[0], nlst.at[0], li_s.at[0], li_r.at[0], after)
    send(lst.at[1], nlst.at[1], li_s.at[1], li_r.at[1], before)
    send(wei, nwei, li_s.at[2], li_r.at[2], after)
    gate, up = joined_gu(0, PARTS)
    hid[0, :, pl.ds(0, FF)] = (gate * jax.nn.sigmoid(gate) * up).astype(BF16)
    product(0)
    collect_early(2)
    exchange_grad(0, *PARTS[0])
    to_mate(0, 0)
    collect_late(2)
    exchange_grad(1, *PARTS[1])
    combine(0, 0)
    gate, up = joined_gu(1, PARTS)
    sg = jax.nn.sigmoid(gate)
    by_gate = up * sg * (1.0 + gate * (1.0 - sg))
    by_up = gate * sg
    joined_grad(0, *PARTS[0])
    joined_grad(1, *PARTS[1])
    grad = (part_g[...] + xr_g[...].astype(F32)).reshape(2 * CHIPS * CAP, FF)
    hid[1, :, pl.ds(0, FF)] = (grad * by_gate).astype(BF16)
    hid[1, :, pl.ds(FF, FF)] = (grad * by_up).astype(BF16)
    product(1)
    to_mate(1, 0)
    combine(1, 0)
    finish(0, 0)
    finish(1, 0)
    for f in range(2):
        until_ready(f, -2)
    for copy in sent:
        copy.wait_send()
    for copy in stores:
        copy.wait()


def per_device(forward_input, saved_input, output_grad, gate_proj, up_proj, down_proj, affinity, token_lists, slot_ids):
    width = forward_input.shape[-1]
    whole = pl.BlockSpec(memory_space=pltpu.HBM)
    blocks = 2 * CHIPS
    entries = blocks * CAP
    dma = pltpu.SemaphoreType.DMA
    rows, spots = pl.pallas_call(
        kernel,
        out_shape=(
            jax.ShapeDtypeStruct((2, EXPERTS, CAP, width), BF16),
            jax.ShapeDtypeStruct((2, 8, TOK), I32),
        ),
        in_specs=[whole] * 9,
        out_specs=(whole, whole),
        scratch_shapes=[
            pltpu.VMEM((2, 1, CHIPS, TOK), F32),
            pltpu.VMEM((2, 1, 1, EXPERTS, CAP), I32),
            pltpu.VMEM((2, 1, 1, EXPERTS, CAP), I32),
            pltpu.VMEM((3, TOK, width), BF16),
            pltpu.VMEM((width, 2 * FF), BF16),
            pltpu.VMEM((FF, width), BF16),
            pltpu.VMEM((3, EXPERTS, CAP, width), BF16),
            pltpu.VMEM((3, 2, CHIPS, CAP, width), BF16),
            pltpu.VMEM((2, 8, TOK), I32),
            pltpu.VMEM((2, 8, TOK), I32),
            pltpu.VMEM((EXPERTS, CAP, TOK), F32),
            pltpu.VMEM((EXPERTS, CAP, TOK), F32),
            pltpu.VMEM((2, CHIPS * CAP, 2 * FF), F32),
            pltpu.VMEM((2, CHIPS * CAP, 2 * FF), F32),
            pltpu.VMEM((2, CHIPS * CAP, FF), F32),
            pltpu.VMEM((2, 2, CHIPS * CAP, 2 * FF), BF16),
            pltpu.VMEM((2, 2, CHIPS * CAP, 2 * FF), BF16),
            pltpu.VMEM((2, CHIPS * CAP, FF), BF16),
            pltpu.VMEM((2, CHIPS * CAP, FF), BF16),
            pltpu.VMEM((2, entries, 2 * FF), BF16),
            pltpu.VMEM((2, CHIPS, CAP, width), BF16),
            pltpu.VMEM((2, CHIPS, CAP, width), BF16),
            pltpu.VMEM((2, CHIPS, CAP, width), F32),
            pltpu.VMEM((2, 4, CAP, width), BF16),
            pltpu.VMEM((2, 4, CAP, width), BF16),
            pltpu.VMEM((2, 4, CAP, width), BF16),
            pltpu.VMEM((2, 4, CAP, width), BF16),
            pltpu.VMEM((2, EXPERTS, CAP, width), BF16),
            dma((9,)), dma((2, 1 + MOST)),
            dma((3, CHIPS)), dma((3, CHIPS)), dma((3, CHIPS)), dma((3, CHIPS)),
            dma((3, 2)), dma((3, 2)), dma((2, MOST, 2)), dma((2, MOST, 2)), dma((2, MOST, 4)), dma((2, MOST, 4)),
            dma((2, MOST, 4)), dma((2, MOST, 4)), dma((3,)), dma((3,)),
            pltpu.SemaphoreType.REGULAR((2 * len(BEYOND),)),
        ],
        compiler_params=pltpu.CompilerParams(
            collective_id=0, has_side_effects=True, vmem_limit_bytes=VMEM_LIMIT
        ),
        cost_estimate=pl.CostEstimate(flops=2_000_000_000, bytes_accessed=6_000_000, transcendentals=262_144),
    )(
        forward_input, saved_input, output_grad, gate_proj, up_proj, down_proj,
        jnp.swapaxes(affinity, 2, 3), token_lists, slot_ids,
    )
    return pl.pallas_call(
        spread,
        out_shape=(jax.ShapeDtypeStruct((1, TOK, width), BF16),) * 2,
        in_specs=[whole] * 2,
        out_specs=(whole, whole),
        scratch_shapes=[
            pltpu.VMEM((2, EXPERTS, CAP, width), BF16),
            pltpu.VMEM((2, 8, TOK), I32),
            pltpu.VMEM((2, TOK, width), BF16),
            dma((3,)), dma((2,)),
        ],
        compiler_params=pltpu.CompilerParams(vmem_limit_bytes=VMEM_LIMIT),
    )(rows, spots)


def solution(mesh):
    in_specs = (
        P("pipe", "expert", "dp"),
        P("pipe", "expert", "dp"),
        P("pipe", "expert", "dp"),
        P("pipe", "dp", "expert"),
        P("pipe", "dp", "expert"),
        P("pipe", "expert", "dp"),
        P(None, "pipe", "expert", None),
        P(None, "pipe", "expert", None, None),
        P(None, "pipe", "expert", None, None),
    )
    out_specs = (P("pipe", "expert", "dp"), P("pipe", "expert", "dp"))
    return jax.shard_map(
        per_device, mesh=mesh, in_specs=in_specs, out_specs=out_specs, check_vma=False
    )
```

```python
import functools

import jax
import jax.numpy as jnp
from jax import lax
from jax.experimental import pallas as pl
from jax.experimental.pallas import tpu as pltpu
from jax.sharding import PartitionSpec as P

MESH = pl.DeviceIdType.MESH
F32, BF16, I32 = jnp.float32, jnp.bfloat16, jnp.int32
ROUTED_SCALE = 2.5
EXPERTS = 2
CAP = 16
TOK = 128
CHIPS = 8
HALF = 4
FF = 256
VMEM_LIMIT = 62 * 1024 * 1024
STEPS = (3, 2, 1)
PEERS = (1, 2, 3, -1, -2)
BEYOND = (0, 1, 2, 3, -2)
MIRROR = {0: 0, 1: 1, 2: -2, 3: 3, -2: 2}
EARLY = 5
SHARES = ((5, 8), (0, 5))
PARTS = ((0, EARLY), (EARLY, CHIPS))
CUTS = (((0, 1792),), ((0, 1792),))
MOST = 2


def dot(a, b, dims, precision=None):
    return lax.dot_general(a, b, ((dims[0], dims[1]), ((), ())), precision=precision, preferred_element_type=F32)


def column(row):
    wide = jnp.broadcast_to(row.astype(F32), (CAP, CAP))
    eye = lax.broadcasted_iota(I32, (CAP, CAP), 0) == lax.broadcasted_iota(I32, (CAP, CAP), 1)
    return jnp.sum(jnp.where(eye, wide, 0.0), axis=1, keepdims=True)


def picker(row):
    lanes = lax.broadcasted_iota(I32, (CAP, TOK), 1).astype(F32)
    return jnp.where(lanes == column(row), 1.0, 0.0)


def placer(row):
    tokens = lax.broadcasted_iota(I32, (TOK, CAP), 0)
    return jnp.where(tokens == jnp.broadcast_to(row, (TOK, CAP)), 1.0, 0.0)


def entry_weight(onehot, slot_row, affinity):
    picked = dot(onehot, affinity, ((1,), (1,)), lax.Precision.HIGHEST)
    slots = lax.broadcasted_iota(I32, (CAP, CHIPS), 1).astype(F32)
    chosen = jnp.sum(jnp.where(slots == column(slot_row), picked, 0.0), axis=1, keepdims=True)
    total = jnp.sum(picked, axis=1, keepdims=True)
    live = total > 0.0
    return jnp.where(live, ROUTED_SCALE * (chosen / jnp.where(live, total, 1.0)), 0.0)


def spread(rows_h, spots_h, out_f, out_b, rows, spots, placed, load_sem, store_sem):
    loads = [
        pltpu.make_async_copy(spots_h, spots, load_sem.at[0]),
        pltpu.make_async_copy(rows_h.at[0], rows.at[0], load_sem.at[1]),
        pltpu.make_async_copy(rows_h.at[1], rows.at[1], load_sem.at[2]),
    ]
    for load in loads:
        load.start()
    loads[0].wait()
    stores = []
    for f, out in enumerate((out_f, out_b)):
        loads[1 + f].wait()
        total = None
        for e in range(EXPERTS):
            spot = placer(spots[f, pl.ds(e, 1), pl.ds(0, CAP)]).astype(BF16)
            term = dot(spot, rows[f, e], ((1,), (0,)))
            total = term if total is None else total + term
        placed[f] = total.astype(BF16)
        stores.append(pltpu.make_async_copy(placed.at[f], out.at[0], store_sem.at[f]))
        stores[f].start()
    for store in stores:
        store.wait()


def kernel(
    fin, sav, gra, wg_h, wu_h, wd_h, aff_h, lists_h, slots_h,
    out_p, out_l,
    aff, lists, slots, vx, wgu, wd, snd, rcv, lst, nlst, wei, nwei,
    part_f, part_b, part_g, xs_gu, xr_gu, xs_g, xr_g,
    hid, sib_s, sib_r, own, mate_s, mate_r, com_s, com_r, ended,
    load_sem, store_sem, dis_s, dis_r, fwd_s, fwd_r, dp_s, dp_r, ss_s, ss_r, ma_s, ma_r, co_s, co_r, li_s, li_r, ready,
):
    p, x, d = lax.axis_index("pipe"), lax.axis_index("expert"), lax.axis_index("dp")
    pipes = lax.axis_size("pipe")
    z, c = lax.div(x, 2), lax.rem(x, 2)
    half = lax.div(z, HALF)
    sibling = (p, z * 2 + 1 - c, d)
    partner = (p, x, 1 - d)
    after = (lax.rem(p + 1, pipes), x, d)
    before = (lax.rem(p + pipes - 1, pipes), x, d)
    toward = 2 * lax.rem(z, 2) - 1
    chip = lambda k: lax.rem(z + CHIPS + k * toward, CHIPS)
    at_chip = lambda k: (p, chip(k) * 2 + c, d)
    goal = {0: 0, 1: 1, 2: -2, 3: 3}
    far = lambda f, k: ((after, before)[f][0], chip(k) * 2 + c, d)
    sent = []

    beyond = [(f, k) for f in range(2) for k in BEYOND]
    higher = (after[0] > p, before[0] > p)

    barrier = pltpu.get_barrier_semaphore()
    for peer in [sibling, partner] + [at_chip(k) for k in PEERS]:
        pl.semaphore_signal(barrier, inc=1, device_id=peer, device_id_type=MESH)
    for f, k in beyond:

        @pl.when(higher[f])
        def _(f=f, k=k):
            pl.semaphore_signal(barrier, inc=1, device_id=far(f, k), device_id_type=MESH)

    def enter():
        lower = 2 - higher[0].astype(I32) - higher[1].astype(I32)
        pl.semaphore_wait(barrier, len(PEERS) + 2 + len(BEYOND) * lower)
        for f, k in beyond:

            @pl.when(jnp.logical_not(higher[f]))
            def _(f=f, k=k):
                i = beyond.index((1 - f, MIRROR[k]))
                pl.semaphore_signal(ready.at[i], inc=1, device_id=far(f, k), device_id_type=MESH)

    def until_ready(f, k):
        @pl.when(higher[f])
        def _():
            pl.semaphore_wait(ready.at[beyond.index((f, k))], 1)

    loads = [
        pltpu.make_async_copy(src, dst, load_sem.at[i])
        for i, (src, dst) in enumerate([
            (fin.at[0], vx.at[0]), (sav.at[0], vx.at[1]), (gra.at[0], vx.at[2]),
            (wg_h.at[0], wgu.at[:, pl.ds(0, FF)]), (wu_h.at[0], wgu.at[:, pl.ds(FF, FF)]), (wd_h.at[0], wd),
            (lists_h, lists), (slots_h, slots), (aff_h, aff),
        ])
    ]
    for i in (6, 0, 1, 7, 8, 2):
        loads[i].start()

    def remote(src, dst, send_sem, recv_sem, device):
        return pltpu.make_async_remote_copy(
            src_ref=src, dst_ref=dst, send_sem=send_sem, recv_sem=recv_sem, device_id=device, device_id_type=MESH
        )

    def send(*args):
        copy = remote(*args)
        copy.start()
        sent.append(copy)

    def pick(f):
        return [picker(lists[f, 0, 0, pl.ds(e, 1), :]) for e in range(EXPERTS)]

    def weigh(f, picks):
        return [entry_weight(picks[e], slots[f, 0, 0, pl.ds(e, 1), :], aff[f, 0]) for e in range(EXPERTS)]

    def gather(a, picks, weights=None):
        got = dot(jnp.concatenate(picks, axis=0).astype(BF16), vx[a], ((1,), (0,)))
        for e in range(EXPERTS):
            block = got[e * CAP : (e + 1) * CAP]
            if weights is not None:
                block = weights[e] * block
            snd[a, e] = block.astype(BF16)
        rcv[a, 0, 0] = snd[a, half]

    def dispatch(a):
        for k in STEPS:
            send(
                snd.at[a, lax.div(chip(goal[k]), HALF)], rcv.at[a, 0, k],
                dis_s.at[a, k], dis_r.at[a, k], at_chip(goal[k]),
            )
        send(snd.at[a, half], rcv.at[a, 0, 4], dis_s.at[a, 4], dis_r.at[a, 4], at_chip(-1))
        share(a, 0)

    def share(a, i):
        send(rcv.at[a, 0, i], rcv.at[a, 1, i], fwd_s.at[a, i], fwd_r.at[a, i], sibling)

    def arrived(a, i):
        remote(snd.at[a, 0], rcv.at[a, 0, i], dis_s.at[a, i], dis_r.at[a, i], sibling).wait_recv()

    def shared(a, first, last):
        for i in range(first, last):
            remote(snd.at[a, 0], rcv.at[a, 1, i], fwd_s.at[a, i], fwd_r.at[a, i], sibling).wait_recv()

    def relay(a, steps=(1, 2, 3)):
        for k in steps:
            arrived(a, k)
            send(rcv.at[a, 0, k], rcv.at[a, 0, 4 + k], dis_s.at[a, 4 + k], dis_r.at[a, 4 + k], at_chip(-1))
            share(a, k)

    def collect_early(a):
        arrived(a, 4)
        share(a, 4)
        shared(a, 0, EARLY)

    def collect_late(a):
        for i in range(EARLY, CHIPS):
            arrived(a, i)
            share(a, i)
        shared(a, EARLY, CHIPS)

    def collect(a):
        arrived(a, 4)
        share(a, 4)
        collect_late(a)
        shared(a, 0, EARLY)

    def all_rows(a):
        return rcv[a].reshape(2 * CHIPS * CAP, rcv.shape[-1])

    loads[6].wait()
    picks = [pick(0)]
    loads[0].wait()
    gather(0, picks[0])
    enter()
    dispatch(0)
    for i in (3, 4, 5):
        loads[i].start()
    picks.append(pick(1))
    loads[1].wait()
    gather(1, picks[1])
    dispatch(1)
    loads[7].wait()
    loads[8].wait()
    loads[2].wait()
    gather(2, picks[1], weigh(1, picks[1]))
    lst[...] = jnp.zeros_like(lst)
    for f in range(2):
        lst[f, pl.ds(0, EXPERTS), pl.ds(0, CAP)] = lists[f, 0, 0]
    weights = weigh(0, picks[0])
    for e in range(EXPERTS):
        wei[e] = jnp.broadcast_to(weights[e], (CAP, TOK))
    for load in loads[3:6]:
        load.wait()

    def exchange_gu(f, i=0, first=0, last=CHIPS):
        part = part_f if f == 0 else part_b
        rows = (last - first) * CAP
        at = pl.ds(first * CAP, rows)
        got = dot(rcv[f, :, pl.ds(first, last - first)].reshape(2 * rows, wd.shape[-1]), wgu[...], ((1,), (0,)))
        got = got.reshape(2, rows, 2 * FF)
        part[:, at, :] = got
        xs_gu[f, :, at, :] = got.astype(BF16)
        send(xs_gu.at[f, :, at], xr_gu.at[f, :, at], dp_s.at[f, i], dp_r.at[f, i], partner)

    def joined_gu(f, parts=((0, CHIPS),)):
        part = part_f if f == 0 else part_b
        for i, (first, last) in enumerate(parts):
            at = pl.ds(first * CAP, (last - first) * CAP)
            remote(xs_gu.at[f, :, at], xr_gu.at[f, :, at], dp_s.at[f, i], dp_r.at[f, i], partner).wait_recv()
        total = (part[...] + xr_gu[f].astype(F32)).reshape(2 * CHIPS * CAP, 2 * FF)
        return total[:, :FF], total[:, FF:]

    def product(f):
        for j, (at, width) in enumerate(CUTS[f]):
            cols = pl.ds(at, width)
            if f == 0:
                got = dot(hid[0, :, pl.ds(0, FF)], wd[:, cols], ((1,), (0,)))
            else:
                got = dot(hid[1], wgu[cols, :], ((1,), (1,)))
            got = got.reshape(2, CHIPS, CAP, width)
            sib_s[f, :, :, cols] = got[1].astype(BF16)
            for i, (first, last) in enumerate(SHARES):
                at = pl.ds(first, last - first)
                send(sib_s.at[f, at, :, cols], sib_r.at[f, at, :, cols], ss_s.at[f, j, i], ss_r.at[f, j, i], sibling)
            own[f, :, :, cols] = got[0]

    def gathered(f, i, cols):
        return own[f, i, :, cols] + sib_r[f, i, :, cols].astype(F32)

    def shared_sum(f, j, i):
        cols = pl.ds(*CUTS[f][j])
        first, last = SHARES[i]
        at = pl.ds(first, last - first)
        remote(
            sib_s.at[f, at, :, cols], sib_r.at[f, at, :, cols], ss_s.at[f, j, i], ss_r.at[f, j, i], sibling
        ).wait_recv()

    def to_mate(f, j):
        cols = pl.ds(*CUTS[f][j])
        for i, (first, last) in enumerate(SHARES[:1]):
            shared_sum(f, j, i)
        for k in STEPS:
            mate_s[f, k, :, cols] = gathered(f, 4 + k, cols).astype(BF16)
            send(mate_s.at[f, k, :, cols], mate_r.at[f, k, :, cols], ma_s.at[f, j, k], ma_r.at[f, j, k], at_chip(-1))

    def mate_own(f, j):
        cols = pl.ds(*CUTS[f][j])
        mate_s[f, 0, :, cols] = gathered(f, 4, cols).astype(BF16)
        send(mate_s.at[f, 0, :, cols], mate_r.at[f, 0, :, cols], ma_s.at[f, j, 0], ma_r.at[f, j, 0], at_chip(-1))

    def from_mate(f, j, k):
        cols = pl.ds(*CUTS[f][j])
        remote(mate_s.at[f, k, :, cols], mate_r.at[f, k, :, cols], ma_s.at[f, j, k], ma_r.at[f, j, k], sibling).wait_recv()
        return (gathered(f, k, cols) + mate_r[f, k, :, cols].astype(F32)).astype(BF16)

    def combine(f, j):
        cols = pl.ds(*CUTS[f][j])
        for k in (1, 2, 3):
            until_ready(f, k)
        pair = lax.div(z, 2)
        shared_sum(f, j, 1)
        for k in STEPS:
            com_s[f, k, :, cols] = from_mate(f, j, k)
            send(com_s.at[f, k, :, cols], com_r.at[f, pair, :, cols], co_s.at[f, j, k], co_r.at[f, j, k], far(f, k))
            if k == STEPS[0]:
                mate_own(f, j)
        com_s[f, 0, :, cols] = from_mate(f, j, 0)
        send(com_s.at[f, 0, :, cols], com_r.at[f, pair, :, cols], co_s.at[f, j, 0], co_r.at[f, j, 0], far(f, 0))

    stores = []

    def finish(f, j):
        cols = pl.ds(*CUTS[f][j])
        if j == 0:
            remote(lst.at[f], nlst.at[f], li_s.at[f], li_r.at[f], after).wait_recv()
            stores.append(pltpu.make_async_copy(nlst.at[f], out_l.at[f], store_sem.at[f, 0]))
            stores[-1].start()
            if f == 0:
                remote(wei, nwei, li_s.at[2], li_r.at[2], after).wait_recv()
        for k in (1, 2, 3, 0):
            source = lax.div(chip(goal[k]), 2)
            remote(
                com_s.at[f, k, :, cols], com_r.at[f, source, :, cols], co_s.at[f, j, k], co_r.at[f, j, k], sibling
            ).wait_recv()
        for e in range(EXPERTS):
            total = com_r[f, 2 * e, :, cols].astype(F32) + com_r[f, 2 * e + 1, :, cols].astype(F32)
            if f == 0:
                total = nwei[e, :, pl.ds(0, 1)] * total
            ended[f, e, :, cols] = total.astype(BF16)
        stores.append(pltpu.make_async_copy(ended.at[f, :, :, cols], out_p.at[f, :, :, cols], store_sem.at[f, 1 + j]))
        stores[-1].start()

    def exchange_grad(i, first, last):
        rows = (last - first) * CAP
        got = dot(rcv[2, :, pl.ds(first, last - first)].reshape(2 * rows, wd.shape[-1]), wd[...], ((1,), (1,)))
        got = got.reshape(2, rows, FF)
        at = pl.ds(first * CAP, rows)
        part_g[:, at, :] = got
        xs_g[:, at, :] = got.astype(BF16)
        send(xs_g.at[:, at], xr_g.at[:, at], dp_s.at[2, i], dp_r.at[2, i], partner)

    def joined_grad(i, first, last):
        at = pl.ds(first * CAP, (last - first) * CAP)
        remote(xs_g.at[:, at], xr_g.at[:, at], dp_s.at[2, i], dp_r.at[2, i], partner).wait_recv()

    relay(0)
    relay(1)
    collect_early(0)
    dispatch(2)
    exchange_gu(0, 0, *PARTS[0])
    collect_late(0)
    exchange_gu(0, 1, *PARTS[1])
    collect_early(1)
    exchange_gu(1, 0, *PARTS[0])
    relay(2)
    collect_late(1)
    exchange_gu(1, 1, *PARTS[1])
    for f in range(2):
        until_ready(f, 0)
    send(lst.at[0], nlst.at[0], li_s.at[0], li_r.at[0], after)
    send(lst.at[1], nlst.at[1], li_s.at[1], li_r.at[1], before)
    send(wei, nwei, li_s.at[2], li_r.at[2], after)
    gate, up = joined_gu(0, PARTS)
    hid[0, :, pl.ds(0, FF)] = (gate * jax.nn.sigmoid(gate) * up).astype(BF16)
    product(0)
    collect_early(2)
    exchange_grad(0, *PARTS[0])
    to_mate(0, 0)
    collect_late(2)
    exchange_grad(1, *PARTS[1])
    combine(0, 0)
    gate, up = joined_gu(1, PARTS)
    sg = jax.nn.sigmoid(gate)
    by_gate = up * sg * (1.0 + gate * (1.0 - sg))
    by_up = gate * sg
    joined_grad(0, *PARTS[0])
    joined_grad(1, *PARTS[1])
    grad = (part_g[...] + xr_g[...].astype(F32)).reshape(2 * CHIPS * CAP, FF)
    hid[1, :, pl.ds(0, FF)] = (grad * by_gate).astype(BF16)
    hid[1, :, pl.ds(FF, FF)] = (grad * by_up).astype(BF16)
    product(1)
    to_mate(1, 0)
    combine(1, 0)
    finish(0, 0)
    finish(1, 0)
    for f in range(2):
        until_ready(f, -2)
    for copy in sent:
        copy.wait_send()
    for copy in stores:
        copy.wait()


def per_device(forward_input, saved_input, output_grad, gate_proj, up_proj, down_proj, affinity, token_lists, slot_ids):
    width = forward_input.shape[-1]
    whole = pl.BlockSpec(memory_space=pltpu.HBM)
    blocks = 2 * CHIPS
    entries = blocks * CAP
    dma = pltpu.SemaphoreType.DMA
    rows, spots = pl.pallas_call(
        kernel,
        out_shape=(
            jax.ShapeDtypeStruct((2, EXPERTS, CAP, width), BF16),
            jax.ShapeDtypeStruct((2, 8, TOK), I32),
        ),
        in_specs=[whole] * 9,
        out_specs=(whole, whole),
        scratch_shapes=[
            pltpu.VMEM((2, 1, CHIPS, TOK), F32),
            pltpu.VMEM((2, 1, 1, EXPERTS, CAP), I32),
            pltpu.VMEM((2, 1, 1, EXPERTS, CAP), I32),
            pltpu.VMEM((3, TOK, width), BF16),
            pltpu.VMEM((width, 2 * FF), BF16),
            pltpu.VMEM((FF, width), BF16),
            pltpu.VMEM((3, EXPERTS, CAP, width), BF16),
            pltpu.VMEM((3, 2, CHIPS, CAP, width), BF16),
            pltpu.VMEM((2, 8, TOK), I32),
            pltpu.VMEM((2, 8, TOK), I32),
            pltpu.VMEM((EXPERTS, CAP, TOK), F32),
            pltpu.VMEM((EXPERTS, CAP, TOK), F32),
            pltpu.VMEM((2, CHIPS * CAP, 2 * FF), F32),
            pltpu.VMEM((2, CHIPS * CAP, 2 * FF), F32),
            pltpu.VMEM((2, CHIPS * CAP, FF), F32),
            pltpu.VMEM((2, 2, CHIPS * CAP, 2 * FF), BF16),
            pltpu.VMEM((2, 2, CHIPS * CAP, 2 * FF), BF16),
            pltpu.VMEM((2, CHIPS * CAP, FF), BF16),
            pltpu.VMEM((2, CHIPS * CAP, FF), BF16),
            pltpu.VMEM((2, entries, 2 * FF), BF16),
            pltpu.VMEM((2, CHIPS, CAP, width), BF16),
            pltpu.VMEM((2, CHIPS, CAP, width), BF16),
            pltpu.VMEM((2, CHIPS, CAP, width), F32),
            pltpu.VMEM((2, 4, CAP, width), BF16),
            pltpu.VMEM((2, 4, CAP, width), BF16),
            pltpu.VMEM((2, 4, CAP, width), BF16),
            pltpu.VMEM((2, 4, CAP, width), BF16),
            pltpu.VMEM((2, EXPERTS, CAP, width), BF16),
            dma((9,)), dma((2, 1 + MOST)),
            dma((3, CHIPS)), dma((3, CHIPS)), dma((3, CHIPS)), dma((3, CHIPS)),
            dma((3, 2)), dma((3, 2)), dma((2, MOST, 2)), dma((2, MOST, 2)), dma((2, MOST, 4)), dma((2, MOST, 4)),
            dma((2, MOST, 4)), dma((2, MOST, 4)), dma((3,)), dma((3,)),
            pltpu.SemaphoreType.REGULAR((2 * len(BEYOND),)),
        ],
        compiler_params=pltpu.CompilerParams(
            collective_id=0, has_side_effects=True, vmem_limit_bytes=VMEM_LIMIT
        ),
        cost_estimate=pl.CostEstimate(flops=2_000_000_000, bytes_accessed=6_000_000, transcendentals=262_144),
    )(
        forward_input, saved_input, output_grad, gate_proj, up_proj, down_proj,
        jnp.swapaxes(affinity, 2, 3), token_lists, slot_ids,
    )
    return pl.pallas_call(
        spread,
        out_shape=(jax.ShapeDtypeStruct((1, TOK, width), BF16),) * 2,
        in_specs=[whole] * 2,
        out_specs=(whole, whole),
        scratch_shapes=[
            pltpu.VMEM((2, EXPERTS, CAP, width), BF16),
            pltpu.VMEM((2, 8, TOK), I32),
            pltpu.VMEM((2, TOK, width), BF16),
            dma((3,)), dma((2,)),
        ],
        compiler_params=pltpu.CompilerParams(vmem_limit_bytes=VMEM_LIMIT),
    )(rows, spots)


def solution(mesh):
    in_specs = (
        P("pipe", "expert", "dp"),
        P("pipe", "expert", "dp"),
        P("pipe", "expert", "dp"),
        P("pipe", "dp", "expert"),
        P("pipe", "dp", "expert"),
        P("pipe", "expert", "dp"),
        P(None, "pipe", "expert", None),
        P(None, "pipe", "expert", None, None),
        P(None, "pipe", "expert", None, None),
    )
    out_specs = (P("pipe", "expert", "dp"), P("pipe", "expert", "dp"))
    return jax.shard_map(
        per_device, mesh=mesh, in_specs=in_specs, out_specs=out_specs, check_vma=False
    )
```

```python
import functools

import jax
import jax.numpy as jnp
from jax import lax
from jax.experimental import pallas as pl
from jax.experimental.pallas import tpu as pltpu
from jax.sharding import PartitionSpec as P

MESH = pl.DeviceIdType.MESH
F32, BF16, I32 = jnp.float32, jnp.bfloat16, jnp.int32
ROUTED_SCALE = 2.5
EXPERTS = 2
CAP = 16
TOK = 128
CHIPS = 8
HALF = 4
FF = 256
VMEM_LIMIT = 62 * 1024 * 1024
STEPS = (3, 2, 1)
PEERS = (1, 2, 3, -1, -2)
BEYOND = (0, 1, 2, 3, -2)
MIRROR = {0: 0, 1: 1, 2: -2, 3: 3, -2: 2}
EARLY = 5
SHARES = ((5, 8), (0, 5))
PARTS = ((0, EARLY), (EARLY, CHIPS))
CUTS = (((0, 1792),), ((0, 1792),))
MOST = 2


def dot(a, b, dims, precision=None):
    return lax.dot_general(a, b, ((dims[0], dims[1]), ((), ())), precision=precision, preferred_element_type=F32)


def column(row):
    wide = jnp.broadcast_to(row.astype(F32), (CAP, CAP))
    eye = lax.broadcasted_iota(I32, (CAP, CAP), 0) == lax.broadcasted_iota(I32, (CAP, CAP), 1)
    return jnp.sum(jnp.where(eye, wide, 0.0), axis=1, keepdims=True)


def picker(row):
    lanes = lax.broadcasted_iota(I32, (CAP, TOK), 1).astype(F32)
    return jnp.where(lanes == column(row), 1.0, 0.0)


def placer(row):
    tokens = lax.broadcasted_iota(I32, (TOK, CAP), 0)
    return jnp.where(tokens == jnp.broadcast_to(row, (TOK, CAP)), 1.0, 0.0)


def entry_weight(onehot, slot_row, affinity):
    picked = dot(onehot, affinity, ((1,), (1,)), lax.Precision.HIGHEST)
    slots = lax.broadcasted_iota(I32, (CAP, CHIPS), 1).astype(F32)
    chosen = jnp.sum(jnp.where(slots == column(slot_row), picked, 0.0), axis=1, keepdims=True)
    total = jnp.sum(picked, axis=1, keepdims=True)
    live = total > 0.0
    return jnp.where(live, ROUTED_SCALE * (chosen / jnp.where(live, total, 1.0)), 0.0)


def spread(rows_h, spots_h, out_f, out_b, rows, spots, placed, load_sem, store_sem):
    loads = [
        pltpu.make_async_copy(spots_h, spots, load_sem.at[0]),
        pltpu.make_async_copy(rows_h.at[0], rows.at[0], load_sem.at[1]),
        pltpu.make_async_copy(rows_h.at[1], rows.at[1], load_sem.at[2]),
    ]
    for load in loads:
        load.start()
    loads[0].wait()
    stores = []
    for f, out in enumerate((out_f, out_b)):
        loads[1 + f].wait()
        total = None
        for e in range(EXPERTS):
            spot = placer(spots[f, pl.ds(e, 1), pl.ds(0, CAP)]).astype(BF16)
            term = dot(spot, rows[f, e], ((1,), (0,)))
            total = term if total is None else total + term
        placed[f] = total.astype(BF16)
        stores.append(pltpu.make_async_copy(placed.at[f], out.at[0], store_sem.at[f]))
        stores[f].start()
    for store in stores:
        store.wait()


def kernel(
    fin, sav, gra, wg_h, wu_h, wd_h, aff_h, lists_h, slots_h,
    out_p, out_l,
    aff, lists, slots, vx, wgu, wd, snd, rcv, lst, nlst, wei, nwei,
    part_f, part_b, part_g, xs_gu, xr_gu, xs_g, xr_g,
    hid, sib_s, sib_r, own, mate_s, mate_r, com_s, com_r, ended,
    load_sem, store_sem, dis_s, dis_r, fwd_s, fwd_r, dp_s, dp_r, ss_s, ss_r, ma_s, ma_r, co_s, co_r, li_s, li_r, ready,
):
    p, x, d = lax.axis_index("pipe"), lax.axis_index("expert"), lax.axis_index("dp")
    pipes = lax.axis_size("pipe")
    z, c = lax.div(x, 2), lax.rem(x, 2)
    half = lax.div(z, HALF)
    sibling = (p, z * 2 + 1 - c, d)
    partner = (p, x, 1 - d)
    after = (lax.rem(p + 1, pipes), x, d)
    before = (lax.rem(p + pipes - 1, pipes), x, d)
    toward = 2 * lax.rem(z, 2) - 1
    chip = lambda k: lax.rem(z + CHIPS + k * toward, CHIPS)
    at_chip = lambda k: (p, chip(k) * 2 + c, d)
    goal = {0: 0, 1: 1, 2: -2, 3: 3}
    far = lambda f, k: ((after, before)[f][0], chip(k) * 2 + c, d)
    sent = []

    beyond = [(f, k) for f in range(2) for k in BEYOND]
    higher = (after[0] > p, before[0] > p)

    barrier = pltpu.get_barrier_semaphore()
    for peer in [sibling, partner] + [at_chip(k) for k in PEERS]:
        pl.semaphore_signal(barrier, inc=1, device_id=peer, device_id_type=MESH)
    for f, k in beyond:

        @pl.when(higher[f])
        def _(f=f, k=k):
            pl.semaphore_signal(barrier, inc=1, device_id=far(f, k), device_id_type=MESH)

    def enter():
        lower = 2 - higher[0].astype(I32) - higher[1].astype(I32)
        pl.semaphore_wait(barrier, len(PEERS) + 2 + len(BEYOND) * lower)
        for f, k in beyond:

            @pl.when(jnp.logical_not(higher[f]))
            def _(f=f, k=k):
                i = beyond.index((1 - f, MIRROR[k]))
                pl.semaphore_signal(ready.at[i], inc=1, device_id=far(f, k), device_id_type=MESH)

    def until_ready(f, k):
        @pl.when(higher[f])
        def _():
            pl.semaphore_wait(ready.at[beyond.index((f, k))], 1)

    loads = [
        pltpu.make_async_copy(src, dst, load_sem.at[i])
        for i, (src, dst) in enumerate([
            (fin.at[0], vx.at[0]), (sav.at[0], vx.at[1]), (gra.at[0], vx.at[2]),
            (wg_h.at[0], wgu.at[:, pl.ds(0, FF)]), (wu_h.at[0], wgu.at[:, pl.ds(FF, FF)]), (wd_h.at[0], wd),
            (lists_h, lists), (slots_h, slots), (aff_h, aff),
        ])
    ]
    for i in (6, 0, 1, 7, 8, 2):
        loads[i].start()

    def remote(src, dst, send_sem, recv_sem, device):
        return pltpu.make_async_remote_copy(
            src_ref=src, dst_ref=dst, send_sem=send_sem, recv_sem=recv_sem, device_id=device, device_id_type=MESH
        )

    def send(*args):
        copy = remote(*args)
        copy.start()
        sent.append(copy)

    def pick(f):
        return [picker(lists[f, 0, 0, pl.ds(e, 1), :]) for e in range(EXPERTS)]

    def weigh(f, picks):
        return [entry_weight(picks[e], slots[f, 0, 0, pl.ds(e, 1), :], aff[f, 0]) for e in range(EXPERTS)]

    def gather(a, picks, weights=None):
        got = dot(jnp.concatenate(picks, axis=0).astype(BF16), vx[a], ((1,), (0,)))
        for e in range(EXPERTS):
            block = got[e * CAP : (e + 1) * CAP]
            if weights is not None:
                block = weights[e] * block
            snd[a, e] = block.astype(BF16)
        rcv[a, 0, 0] = snd[a, half]

    def dispatch(a):
        for k in STEPS:
            send(
                snd.at[a, lax.div(chip(goal[k]), HALF)], rcv.at[a, 0, k],
                dis_s.at[a, k], dis_r.at[a, k], at_chip(goal[k]),
            )
        send(snd.at[a, half], rcv.at[a, 0, 4], dis_s.at[a, 4], dis_r.at[a, 4], at_chip(-1))
        share(a, 0)

    def share(a, i):
        send(rcv.at[a, 0, i], rcv.at[a, 1, i], fwd_s.at[a, i], fwd_r.at[a, i], sibling)

    def arrived(a, i):
        remote(snd.at[a, 0], rcv.at[a, 0, i], dis_s.at[a, i], dis_r.at[a, i], sibling).wait_recv()

    def shared(a, first, last):
        for i in range(first, last):
            remote(snd.at[a, 0], rcv.at[a, 1, i], fwd_s.at[a, i], fwd_r.at[a, i], sibling).wait_recv()

    def relay(a, steps=(1, 2, 3)):
        for k in steps:
            arrived(a, k)
            send(rcv.at[a, 0, k], rcv.at[a, 0, 4 + k], dis_s.at[a, 4 + k], dis_r.at[a, 4 + k], at_chip(-1))
            share(a, k)

    def collect_early(a):
        arrived(a, 4)
        share(a, 4)
        shared(a, 0, EARLY)

    def collect_late(a):
        for i in range(EARLY, CHIPS):
            arrived(a, i)
            share(a, i)
        shared(a, EARLY, CHIPS)

    def collect(a):
        arrived(a, 4)
        share(a, 4)
        collect_late(a)
        shared(a, 0, EARLY)

    def all_rows(a):
        return rcv[a].reshape(2 * CHIPS * CAP, rcv.shape[-1])

    loads[6].wait()
    picks = [pick(0)]
    loads[0].wait()
    gather(0, picks[0])
    enter()
    dispatch(0)
    for i in (3, 4, 5):
        loads[i].start()
    picks.append(pick(1))
    loads[1].wait()
    gather(1, picks[1])
    dispatch(1)
    for load in loads[3:6]:
        load.wait()

    def exchange_gu(f, i=0, first=0, last=CHIPS):
        part = part_f if f == 0 else part_b
        rows = (last - first) * CAP
        at = pl.ds(first * CAP, rows)
        got = dot(rcv[f, :, pl.ds(first, last - first)].reshape(2 * rows, wd.shape[-1]), wgu[...], ((1,), (0,)))
        got = got.reshape(2, rows, 2 * FF)
        part[:, at, :] = got
        xs_gu[f, :, at, :] = got.astype(BF16)
        send(xs_gu.at[f, :, at], xr_gu.at[f, :, at], dp_s.at[f, i], dp_r.at[f, i], partner)

    def joined_gu(f, parts=((0, CHIPS),)):
        part = part_f if f == 0 else part_b
        for i, (first, last) in enumerate(parts):
            at = pl.ds(first * CAP, (last - first) * CAP)
            remote(xs_gu.at[f, :, at], xr_gu.at[f, :, at], dp_s.at[f, i], dp_r.at[f, i], partner).wait_recv()
        total = (part[...] + xr_gu[f].astype(F32)).reshape(2 * CHIPS * CAP, 2 * FF)
        return total[:, :FF], total[:, FF:]

    def product(f):
        for j, (at, width) in enumerate(CUTS[f]):
            cols = pl.ds(at, width)
            if f == 0:
                got = dot(hid[0, :, pl.ds(0, FF)], wd[:, cols], ((1,), (0,)))
            else:
                got = dot(hid[1], wgu[cols, :], ((1,), (1,)))
            got = got.reshape(2, CHIPS, CAP, width)
            sib_s[f, :, :, cols] = got[1].astype(BF16)
            for i, (first, last) in enumerate(SHARES):
                at = pl.ds(first, last - first)
                send(sib_s.at[f, at, :, cols], sib_r.at[f, at, :, cols], ss_s.at[f, j, i], ss_r.at[f, j, i], sibling)
            own[f, :, :, cols] = got[0]

    def gathered(f, i, cols):
        return own[f, i, :, cols] + sib_r[f, i, :, cols].astype(F32)

    def shared_sum(f, j, i):
        cols = pl.ds(*CUTS[f][j])
        first, last = SHARES[i]
        at = pl.ds(first, last - first)
        remote(
            sib_s.at[f, at, :, cols], sib_r.at[f, at, :, cols], ss_s.at[f, j, i], ss_r.at[f, j, i], sibling
        ).wait_recv()

    def to_mate(f, j):
        cols = pl.ds(*CUTS[f][j])
        for i, (first, last) in enumerate(SHARES[:1]):
            shared_sum(f, j, i)
        for k in STEPS:
            mate_s[f, k, :, cols] = gathered(f, 4 + k, cols).astype(BF16)
            send(mate_s.at[f, k, :, cols], mate_r.at[f, k, :, cols], ma_s.at[f, j, k], ma_r.at[f, j, k], at_chip(-1))

    def mate_own(f, j):
        cols = pl.ds(*CUTS[f][j])
        mate_s[f, 0, :, cols] = gathered(f, 4, cols).astype(BF16)
        send(mate_s.at[f, 0, :, cols], mate_r.at[f, 0, :, cols], ma_s.at[f, j, 0], ma_r.at[f, j, 0], at_chip(-1))

    def from_mate(f, j, k):
        cols = pl.ds(*CUTS[f][j])
        remote(mate_s.at[f, k, :, cols], mate_r.at[f, k, :, cols], ma_s.at[f, j, k], ma_r.at[f, j, k], sibling).wait_recv()
        return (gathered(f, k, cols) + mate_r[f, k, :, cols].astype(F32)).astype(BF16)

    def combine(f, j):
        cols = pl.ds(*CUTS[f][j])
        for k in (1, 2, 3):
            until_ready(f, k)
        pair = lax.div(z, 2)
        shared_sum(f, j, 1)
        for k in STEPS:
            com_s[f, k, :, cols] = from_mate(f, j, k)
            send(com_s.at[f, k, :, cols], com_r.at[f, pair, :, cols], co_s.at[f, j, k], co_r.at[f, j, k], far(f, k))
            if k == STEPS[0]:
                mate_own(f, j)
        com_s[f, 0, :, cols] = from_mate(f, j, 0)
        send(com_s.at[f, 0, :, cols], com_r.at[f, pair, :, cols], co_s.at[f, j, 0], co_r.at[f, j, 0], far(f, 0))

    stores = []

    def finish(f, j):
        cols = pl.ds(*CUTS[f][j])
        if j == 0:
            remote(lst.at[f], nlst.at[f], li_s.at[f], li_r.at[f], after).wait_recv()
            stores.append(pltpu.make_async_copy(nlst.at[f], out_l.at[f], store_sem.at[f, 0]))
            stores[-1].start()
            if f == 0:
                remote(wei, nwei, li_s.at[2], li_r.at[2], after).wait_recv()
        for k in (1, 2, 3, 0):
            source = lax.div(chip(goal[k]), 2)
            remote(
                com_s.at[f, k, :, cols], com_r.at[f, source, :, cols], co_s.at[f, j, k], co_r.at[f, j, k], sibling
            ).wait_recv()
        for e in range(EXPERTS):
            total = com_r[f, 2 * e, :, cols].astype(F32) + com_r[f, 2 * e + 1, :, cols].astype(F32)
            if f == 0:
                total = nwei[e, :, pl.ds(0, 1)] * total
            ended[f, e, :, cols] = total.astype(BF16)
        stores.append(pltpu.make_async_copy(ended.at[f, :, :, cols], out_p.at[f, :, :, cols], store_sem.at[f, 1 + j]))
        stores[-1].start()

    def exchange_grad(i, first, last):
        rows = (last - first) * CAP
        got = dot(rcv[2, :, pl.ds(first, last - first)].reshape(2 * rows, wd.shape[-1]), wd[...], ((1,), (1,)))
        got = got.reshape(2, rows, FF)
        at = pl.ds(first * CAP, rows)
        part_g[:, at, :] = got
        xs_g[:, at, :] = got.astype(BF16)
        send(xs_g.at[:, at], xr_g.at[:, at], dp_s.at[2, i], dp_r.at[2, i], partner)

    def joined_grad(i, first, last):
        at = pl.ds(first * CAP, (last - first) * CAP)
        remote(xs_g.at[:, at], xr_g.at[:, at], dp_s.at[2, i], dp_r.at[2, i], partner).wait_recv()

    relay(0)
    loads[7].wait()
    loads[8].wait()
    loads[2].wait()
    gather(2, picks[1], weigh(1, picks[1]))
    relay(1)
    collect_early(0)
    dispatch(2)
    exchange_gu(0, 0, *PARTS[0])
    collect_late(0)
    exchange_gu(0, 1, *PARTS[1])
    collect_early(1)
    exchange_gu(1, 0, *PARTS[0])
    relay(2)
    collect_late(1)
    exchange_gu(1, 1, *PARTS[1])
    lst[...] = jnp.zeros_like(lst)
    for f in range(2):
        lst[f, pl.ds(0, EXPERTS), pl.ds(0, CAP)] = lists[f, 0, 0]
    weights = weigh(0, picks[0])
    for e in range(EXPERTS):
        wei[e] = jnp.broadcast_to(weights[e], (CAP, TOK))
    for f in range(2):
        until_ready(f, 0)
    send(lst.at[0], nlst.at[0], li_s.at[0], li_r.at[0], after)
    send(lst.at[1], nlst.at[1], li_s.at[1], li_r.at[1], before)
    send(wei, nwei, li_s.at[2], li_r.at[2], after)
    gate, up = joined_gu(0, PARTS)
    hid[0, :, pl.ds(0, FF)] = (gate * jax.nn.sigmoid(gate) * up).astype(BF16)
    product(0)
    collect_early(2)
    exchange_grad(0, *PARTS[0])
    to_mate(0, 0)
    collect_late(2)
    exchange_grad(1, *PARTS[1])
    combine(0, 0)
    gate, up = joined_gu(1, PARTS)
    sg = jax.nn.sigmoid(gate)
    by_gate = up * sg * (1.0 + gate * (1.0 - sg))
    by_up = gate * sg
    joined_grad(0, *PARTS[0])
    joined_grad(1, *PARTS[1])
    grad = (part_g[...] + xr_g[...].astype(F32)).reshape(2 * CHIPS * CAP, FF)
    hid[1, :, pl.ds(0, FF)] = (grad * by_gate).astype(BF16)
    hid[1, :, pl.ds(FF, FF)] = (grad * by_up).astype(BF16)
    product(1)
    to_mate(1, 0)
    combine(1, 0)
    finish(0, 0)
    finish(1, 0)
    for f in range(2):
        until_ready(f, -2)
    for copy in sent:
        copy.wait_send()
    for copy in stores:
        copy.wait()


def per_device(forward_input, saved_input, output_grad, gate_proj, up_proj, down_proj, affinity, token_lists, slot_ids):
    width = forward_input.shape[-1]
    whole = pl.BlockSpec(memory_space=pltpu.HBM)
    blocks = 2 * CHIPS
    entries = blocks * CAP
    dma = pltpu.SemaphoreType.DMA
    rows, spots = pl.pallas_call(
        kernel,
        out_shape=(
            jax.ShapeDtypeStruct((2, EXPERTS, CAP, width), BF16),
            jax.ShapeDtypeStruct((2, 8, TOK), I32),
        ),
        in_specs=[whole] * 9,
        out_specs=(whole, whole),
        scratch_shapes=[
            pltpu.VMEM((2, 1, CHIPS, TOK), F32),
            pltpu.VMEM((2, 1, 1, EXPERTS, CAP), I32),
            pltpu.VMEM((2, 1, 1, EXPERTS, CAP), I32),
            pltpu.VMEM((3, TOK, width), BF16),
            pltpu.VMEM((width, 2 * FF), BF16),
            pltpu.VMEM((FF, width), BF16),
            pltpu.VMEM((3, EXPERTS, CAP, width), BF16),
            pltpu.VMEM((3, 2, CHIPS, CAP, width), BF16),
            pltpu.VMEM((2, 8, TOK), I32),
            pltpu.VMEM((2, 8, TOK), I32),
            pltpu.VMEM((EXPERTS, CAP, TOK), F32),
            pltpu.VMEM((EXPERTS, CAP, TOK), F32),
            pltpu.VMEM((2, CHIPS * CAP, 2 * FF), F32),
            pltpu.VMEM((2, CHIPS * CAP, 2 * FF), F32),
            pltpu.VMEM((2, CHIPS * CAP, FF), F32),
            pltpu.VMEM((2, 2, CHIPS * CAP, 2 * FF), BF16),
            pltpu.VMEM((2, 2, CHIPS * CAP, 2 * FF), BF16),
            pltpu.VMEM((2, CHIPS * CAP, FF), BF16),
            pltpu.VMEM((2, CHIPS * CAP, FF), BF16),
            pltpu.VMEM((2, entries, 2 * FF), BF16),
            pltpu.VMEM((2, CHIPS, CAP, width), BF16),
            pltpu.VMEM((2, CHIPS, CAP, width), BF16),
            pltpu.VMEM((2, CHIPS, CAP, width), F32),
            pltpu.VMEM((2, 4, CAP, width), BF16),
            pltpu.VMEM((2, 4, CAP, width), BF16),
            pltpu.VMEM((2, 4, CAP, width), BF16),
            pltpu.VMEM((2, 4, CAP, width), BF16),
            pltpu.VMEM((2, EXPERTS, CAP, width), BF16),
            dma((9,)), dma((2, 1 + MOST)),
            dma((3, CHIPS)), dma((3, CHIPS)), dma((3, CHIPS)), dma((3, CHIPS)),
            dma((3, 2)), dma((3, 2)), dma((2, MOST, 2)), dma((2, MOST, 2)), dma((2, MOST, 4)), dma((2, MOST, 4)),
            dma((2, MOST, 4)), dma((2, MOST, 4)), dma((3,)), dma((3,)),
            pltpu.SemaphoreType.REGULAR((2 * len(BEYOND),)),
        ],
        compiler_params=pltpu.CompilerParams(
            collective_id=0, has_side_effects=True, vmem_limit_bytes=VMEM_LIMIT
        ),
        cost_estimate=pl.CostEstimate(flops=2_000_000_000, bytes_accessed=6_000_000, transcendentals=262_144),
    )(
        forward_input, saved_input, output_grad, gate_proj, up_proj, down_proj,
        jnp.swapaxes(affinity, 2, 3), token_lists, slot_ids,
    )
    return pl.pallas_call(
        spread,
        out_shape=(jax.ShapeDtypeStruct((1, TOK, width), BF16),) * 2,
        in_specs=[whole] * 2,
        out_specs=(whole, whole),
        scratch_shapes=[
            pltpu.VMEM((2, EXPERTS, CAP, width), BF16),
            pltpu.VMEM((2, 8, TOK), I32),
            pltpu.VMEM((2, TOK, width), BF16),
            dma((3,)), dma((2,)),
        ],
        compiler_params=pltpu.CompilerParams(vmem_limit_bytes=VMEM_LIMIT),
    )(rows, spots)


def solution(mesh):
    in_specs = (
        P("pipe", "expert", "dp"),
        P("pipe", "expert", "dp"),
        P("pipe", "expert", "dp"),
        P("pipe", "dp", "expert"),
        P("pipe", "dp", "expert"),
        P("pipe", "expert", "dp"),
        P(None, "pipe", "expert", None),
        P(None, "pipe", "expert", None, None),
        P(None, "pipe", "expert", None, None),
    )
    out_specs = (P("pipe", "expert", "dp"), P("pipe", "expert", "dp"))
    return jax.shard_map(
        per_device, mesh=mesh, in_specs=in_specs, out_specs=out_specs, check_vma=False
    )
```
